256 devices in a mesh: dp: 16 (over z, core), expert: 16 (over x, y).
Axes of the slice: x: 4, y: 4, z: 8, core: 2. Of those that a mesh axis runs over, the one named last changes fastest.
Arguments:
- tokens: bfloat16 [2048, 1440], P('expert'), may hold values from -6 to 6
- output_grad: bfloat16 [2048, 1440], P('expert'), may hold values from -6 to 6
- router_logits: float32 [2048, 4], P('expert'), may hold values from -4 to 4
- expert_ids: int32 [2048, 4], P('expert'), may hold values from 0 to 63, all different within a row; in each aligned block of 128 rows (0 to 127, 128 to 255, ...) at most 10 rows name the same one
- w_gate: bfloat16 [64, 1440, 2048], P('expert', None, 'dp'), may hold values from -0.21875 to 0.21875
- w_up: bfloat16 [64, 1440, 2048], P('expert', None, 'dp'), may hold values from -0.21875 to 0.21875
- w_down: bfloat16 [64, 2048, 1440], P('expert', 'dp'), may hold values from -0.1875 to 0.1875
Outputs:
- mixed: bfloat16 [2048, 1440], P('expert', 'dp')
- input_grad: bfloat16 [2048, 1440], P('expert', 'dp')
- router_grad: float32 [2048, 4], P('expert')
- grad_gate: bfloat16 [64, 1440, 2048], P('expert', None, 'dp')
- grad_up: bfloat16 [64, 1440, 2048], P('expert', None, 'dp')
- grad_down: bfloat16 [64, 2048, 1440], P('expert', 'dp')
The draws below stay inside these ranges and needn't reach their ends.
Inputs may be any that keep to these rules, and one draw needn't show every extreme that they name: `expert_ids`: in each aligned block of 128 rows (the rows of one device), no expert is named more than 10 times, a bound that some block reaches.
All inputs are finite; a program needn't handle non-finite values.
Results may differ from the reference program's by a relative error of at most 0.0064.
Values may be sent and summed in bfloat16 or wider, within the bound.
A program may use at most 128 MiB of HBM per device.

```python
import math
import jax
import jax.numpy as jnp
import numpy as np
from jax import lax

D = 1440
FF = 2048
TOPK = 4
TOK_DEV = 128
EXPERTS = 64
CAP = 10
TOKENS = 2048
N_EXPERT = 16


def spiked(array, key, source, target, blocks, factor):
    owner, partner = [(jnp.arange(array.shape[position]) // (array.shape[position] // blocks)).reshape([-1 if axis == position else 1 for axis in range(array.ndim)]) for position in (source, target)]
    chosen = jax.random.permutation(key, blocks)[partner]
    strong = (owner == chosen) | (owner == (partner + blocks // 2) % blocks)
    return jnp.where(strong, factor * array, array)


def shard_levels(rng, extent, cuts, smallest, largest):
    gain = 1.0
    for dim, parts in cuts:
        steps = jax.random.uniform(jax.random.fold_in(jax.random.fold_in(rng, 6), dim), (parts,), jnp.float32, smallest / len(cuts), largest / len(cuts))
        gain = gain * jnp.repeat(jnp.exp(steps), extent[dim] // parts).reshape((-1,) + (1,) * (len(extent) - 1 - dim))
    return gain


def assign_block(own_key, own, number, rows, count, top, limit, lean):
    order = jax.random.permutation(own_key, count)
    packed, common = shares(count, rows * top, limit, lean, True), shares(count, rows * top, limit, lean, False)
    places = jnp.arange(count)

    def named(tallies, turn):
        used = int((tallies > 0).sum())
        fixed = max(1, used // 4)
        moved = fixed + (places - fixed + turn * (used - fixed)) % max(1, count - fixed)
        return jnp.zeros((count,), jnp.int32).at[order[jnp.where(places < fixed, places, moved)]].set(jnp.asarray(tallies, jnp.int32))

    tallies = jnp.where(number % 4 == 0, named(packed, number // 4), named(common, number - number // 4 - 1))
    mixed = jax.random.permutation(jax.random.fold_in(own, 3), count)
    donor, sink = mixed[0:count // 2 * 2:2], mixed[1:count // 2 * 2:2]
    room = jnp.minimum(tallies[donor] - 1, limit - tallies[sink]) // 2
    room = jnp.where((donor == order[0]) | (sink == order[0]) | (tallies[sink] == 0), 0, jnp.maximum(room, 0))
    moved = jax.random.randint(jax.random.fold_in(own, 4), (count // 2,), 0, 1 << 20) % (room + 1)
    tallies = tallies.at[donor].add(-moved).at[sink].add(moved)
    labels = jnp.searchsorted(jnp.cumsum(tallies), jnp.arange(rows * top), side="right").astype(jnp.int32)
    grid = labels.reshape(top, rows).T
    grid = grid[jax.random.permutation(jax.random.fold_in(own, 1), rows)]
    turn = jax.random.randint(jax.random.fold_in(own, 2), (rows, 1), 0, top)
    return jnp.take_along_axis(grid, (jnp.arange(top)[None, :] + turn) % top, axis=1)


def shares(count, total, bound, skew, full):
    portions = [(1 << 20) // math.isqrt(rank ** skew) + 1 for rank in range(1, count + 1)]
    largest = bound if full else min(bound, max(-(-total // count), total * portions[0] // sum(portions)))
    least = 1 if total - largest >= count - 1 else 0
    given, spare = [largest] + [least] * (count - 1), total - largest - least * (count - 1)
    while spare > 0:
        candidates = [i for i in range(1, count) if given[i] < largest] or [i for i in range(1, count) if given[i] < bound]
        mass, budget = sum([portions[i] for i in candidates]), spare
        for i in candidates:
            addition = min(bound - given[i], max(1, budget * portions[i] // mass), spare)
            given[i] = given[i] + addition
            spare = spare - addition
    return np.array(given)


def gaussian(key, shape, spread, most, split=(), kind=jnp.bfloat16):
    level = shard_levels(key, shape, split, -0.22, 0.18) if split else 1.0
    drawn = jax.random.normal(key, shape, jnp.float32) * spread * level
    return jnp.minimum(jnp.maximum(drawn, -most), most).astype(kind)


def bell_draw_with(stream_key, extent, deviation, bound, cuts, heavy, kind=jnp.bfloat16):
    drawn = deviation * jax.random.normal(stream_key, extent, jnp.float32)
    if cuts:
        drawn = drawn * shard_levels(stream_key, extent, cuts, -0.22, 0.18)
    return jnp.clip(spiked(drawn, jax.random.fold_in(stream_key, 3), *heavy), -bound, bound).astype(kind)


def setup_inputs(seed: int = 0) -> dict:
    keys = jax.random.split(jax.random.key(seed), 8)
    tokens = gaussian(keys[0], (TOKENS, D), 1.0, 6.0, ((0, 16),))
    output_grad = gaussian(keys[1], (TOKENS, D), 1.0, 6.0, ((0, 16),))
    router_logits = gaussian(keys[2], (TOKENS, TOPK), 1.0, 4.0, ((0, 16),), jnp.float32)
    expert_ids_keys = jax.random.split(jax.random.fold_in(keys[3], 1), TOKENS // TOK_DEV)
    expert_ids_turns = jax.random.permutation(jax.random.fold_in(keys[3], 3), TOKENS // TOK_DEV)
    expert_ids = jax.vmap(lambda own, number: assign_block(jax.random.fold_in(keys[3], 2), own, number, TOK_DEV, EXPERTS, TOPK, CAP, 2))(expert_ids_keys, expert_ids_turns).reshape((TOKENS, TOPK))
    w_gate = bell_draw_with(keys[4], (EXPERTS, D, FF), D ** -0.5, 0.21875, ((0, 16), (2, 16)), (2, 1, 16, 2.0))
    w_up = bell_draw_with(keys[5], (EXPERTS, D, FF), D ** -0.5, 0.21875, ((0, 16), (2, 16)), (2, 1, 16, 2.0))
    w_down = bell_draw_with(keys[6], (EXPERTS, FF, D), FF ** -0.5, 0.1875, ((0, 16), (1, 16)), (1, 2, 16, 2.0))
    return {"tokens": tokens, "output_grad": output_grad, "router_logits": router_logits, "expert_ids": expert_ids, "w_gate": w_gate, "w_up": w_up, "w_down": w_down}


def block_ranks(block_ids):
    one_hot = (block_ids[:, None] == jnp.arange(EXPERTS, dtype=jnp.int32)[None, :]).astype(jnp.int32)
    before = jnp.cumsum(one_hot, 0) - one_hot
    return jnp.sum(before * one_hot, 1).astype(jnp.int32)


def reference(tokens, output_grad, router_logits, expert_ids, w_gate, w_up, w_down):
    lifted = jnp.exp(router_logits)
    weights = lifted / jnp.sum(lifted, -1, keepdims=True)
    flat_ids = expert_ids.reshape(-1).astype(jnp.int32)
    num_picks = TOKENS * TOPK
    pick_rank = jax.vmap(block_ranks)(flat_ids.reshape(N_EXPERT, TOK_DEV * TOPK)).reshape(-1)
    source = jnp.arange(num_picks, dtype=jnp.int32) // (TOK_DEV * TOPK)
    slot_of = (flat_ids * (N_EXPERT * CAP) + source * CAP + pick_rank).astype(jnp.int32)
    slot_table = jnp.full((EXPERTS * N_EXPERT * CAP,), num_picks, jnp.int32)
    slot_table = slot_table.at[slot_of].set(jnp.arange(num_picks, dtype=jnp.int32))
    zero_row = jnp.zeros((1, D), jnp.bfloat16)
    x_pick = jnp.concatenate([jnp.repeat(tokens, TOPK, axis=0), zero_row], 0)
    scaled = weights.reshape(-1, 1) * jnp.repeat(output_grad, TOPK, axis=0).astype(jnp.float32)
    g_pick = jnp.concatenate([scaled.astype(jnp.bfloat16), zero_row], 0)

    def expert_pass(expert_item):
        row_index, gate_w, up_w, down_w = expert_item
        rows_in = x_pick[row_index]
        grads_in = g_pick[row_index]
        pre_gate = jnp.dot(rows_in, gate_w, preferred_element_type=jnp.float32)
        pre_up = jnp.dot(rows_in, up_w, preferred_element_type=jnp.float32)
        sigmoid_gate = jax.nn.sigmoid(1.702 * pre_gate)
        activated = pre_gate * sigmoid_gate
        hidden = (activated * (pre_up + 1.0)).astype(jnp.bfloat16)
        expert_out = jnp.dot(hidden, down_w, preferred_element_type=jnp.float32).astype(jnp.bfloat16)
        hidden_grad = jnp.dot(grads_in, down_w.T, preferred_element_type=jnp.float32)
        slope = sigmoid_gate + 1.702 * pre_gate * sigmoid_gate * (1.0 - sigmoid_gate)
        gate_grad = (hidden_grad * (pre_up + 1.0) * slope).astype(jnp.bfloat16)
        up_grad = (hidden_grad * activated).astype(jnp.bfloat16)
        down_total = jnp.dot(hidden.T, grads_in, preferred_element_type=jnp.float32).astype(jnp.bfloat16)
        gate_total = jnp.dot(rows_in.T, gate_grad, preferred_element_type=jnp.float32).astype(jnp.bfloat16)
        up_total = jnp.dot(rows_in.T, up_grad, preferred_element_type=jnp.float32).astype(jnp.bfloat16)
        slot_grad = (jnp.dot(gate_grad, gate_w.T, preferred_element_type=jnp.float32)
                     + jnp.dot(up_grad, up_w.T, preferred_element_type=jnp.float32)).astype(jnp.bfloat16)
        return expert_out, slot_grad, gate_total, up_total, down_total

    expert_out, slot_grad, grad_gate, grad_up, grad_down = lax.map(
        expert_pass, (slot_table.reshape(EXPERTS, N_EXPERT * CAP), w_gate, w_up, w_down))
    out_pick = expert_out.reshape(-1, D)[slot_of].reshape(TOKENS, TOPK, D).astype(jnp.float32)
    mixed = jnp.sum(weights[:, :, None] * out_pick, 1).astype(jnp.bfloat16)
    pick_dot = jnp.sum(output_grad.astype(jnp.float32)[:, None, :] * out_pick, -1)
    router_grad = weights * (pick_dot - jnp.sum(weights * pick_dot, -1, keepdims=True))
    grad_pick = slot_grad.reshape(-1, D)[slot_of].reshape(TOKENS, TOPK, D).astype(jnp.float32)
    input_grad = jnp.sum(grad_pick, 1).astype(jnp.bfloat16)
    return mixed, input_grad, router_grad, grad_gate, grad_up, grad_down
```

```python
import functools

import jax
import jax.numpy as jnp
from jax import lax
from jax.experimental import pallas as pl
from jax.experimental.pallas import tpu as pltpu
from jax.sharding import PartitionSpec as P

MESH = pl.DeviceIdType.MESH
F32 = jnp.float32
BF16 = jnp.bfloat16

D = 1440
HALF = 720
WIDE = 768
PADDED = 1536
HID = 128
TOK = 128
RANKS = 10
SRC = 16
ROWS = SRC * RANKS
PAIR = 2 * ROWS
SLAB = 16
MSG = 1024
GROUP = 256
BLK = 90
BROWS = 96


def dg(a, b, ca, cb):
    return lax.dot_general(a, b, (((ca,), (cb,)), ((), ())), preferred_element_type=F32)


def iota(shape, dim):
    return lax.broadcasted_iota(jnp.int32, shape, dim)


def ones_where(mask):
    return jnp.where(mask, 1.0, 0.0).astype(BF16)


def kernel(
    tok_hbm, og_hbm, logits_ref, ids_ref, wg_hbm, wu_hbm, wd_hbm,
    mixed_ref, igrad_ref, rgrad_ref, gg_hbm, gu_hbm, gd_hbm,
    tok, og, wg, wu, wd,
    send_slab, cat, rows, sel_main, sel_fold, comb_hi, comb_lo, comb_one,
    grp, ungrp, blksel,
    sig, pre, act, upp, hid, ggu,
    part, crecv, zsend, zrecv, slab, back, blocks, frecv, dots,
    grads,
    in_sem, xy_s, xy_r, zf_s, zf_r, cf_s, cf_r, rc_s, rc_r, rz_s, rz_r,
    bk_s, bk_r, fb_s, fb_r, dt_s, dt_r, out_sem,
):
    d = lax.axis_index("dp")
    me = lax.axis_index("expert")
    z, c = lax.div(d, 2), lax.rem(d, 2)
    x, y = lax.div(me, 4), lax.rem(me, 4)
    par = lax.rem(z, 2)
    sib = (z * 2 + 1 - c, me)
    up = (lax.rem(z + 1, 8) * 2 + c, me)
    down = (lax.rem(z + 7, 8) * 2 + c, me)

    def peer(i):
        return lax.rem(x + i // 4, 4) * 4 + lax.rem(y + i % 4, 4)

    def origin(i):
        return lax.rem(x + 4 - i // 4, 4) * 4 + lax.rem(y + 4 - i % 4, 4)

    def slab_rows(s):
        return pl.ds(pl.multiple_of(s * SLAB, SLAB), SLAB)

    barrier = pltpu.get_barrier_semaphore()

    def greet(i, carry):
        pl.semaphore_signal(barrier, inc=1, device_id=(d, peer(i)), device_id_type=MESH)
        pl.semaphore_signal(
            barrier, inc=1, device_id=(lax.rem(d + i, 16), me), device_id_type=MESH
        )
        return carry

    lax.fori_loop(1, 16, greet, 0)

    loads = [
        pltpu.make_async_copy(tok_hbm, tok.at[pl.ds(0, D)], in_sem.at[0]),
        pltpu.make_async_copy(og_hbm, og.at[pl.ds(0, D)], in_sem.at[1]),
    ]
    for n, (src, dst) in enumerate(((wg_hbm, wg), (wu_hbm, wu), (wd_hbm, wd))):
        for e in range(4):
            loads.append(
                pltpu.make_async_copy(src.at[e], dst.at[e, pl.ds(0, D)], in_sem.at[2 + 4 * n + e])
            )
    for load in loads:
        load.start()
    tok[pl.ds(D, PADDED - D), :] = jnp.zeros((PADDED - D, TOK), BF16)
    og[pl.ds(D, PADDED - D), :] = jnp.zeros((PADDED - D, TOK), BF16)
    for w in (wg, wu, wd):
        for e in range(4):
            w[e, pl.ds(D, WIDE - HALF), :] = jnp.zeros((WIDE - HALF, HID), BF16)

    lifted = jnp.exp(logits_ref[...])
    weights = lifted / jnp.sum(lifted, 0, keepdims=True)
    ids = ids_ref[...]
    row = iota((256, TOK), 0)
    spot = row & 15
    earlier = ones_where(iota((TOK, TOK), 0) < iota((TOK, TOK), 1))

    def select(expert, rank):
        named = jnp.zeros((256, TOK), F32)
        weigh = jnp.zeros((256, TOK), F32)
        for p in range(4):
            same = ids[p : p + 1, :] == expert
            named = jnp.where(same, 1.0, named)
            weigh = jnp.where(same, weights[p : p + 1, :], weigh)
        before = dg(named.astype(BF16), earlier, 1, 0)
        chosen = (before == rank.astype(F32)) & (named > 0.5)
        return chosen, jnp.where(chosen, weigh, 0.0)

    second = jnp.where(spot >= RANKS, 1, 0)
    base = 4 * (row >> 4) + 2 * par
    main_expert = base + second
    fold_expert = base + 1
    main, main_w = select(main_expert, spot - RANKS * second)
    fold, fold_w = select(fold_expert, 6 + (spot & 3))
    sel_main[...] = ones_where(main)
    comb_hi[0] = main_w.astype(BF16)
    comb_lo[0] = (main_w - main_w.astype(BF16).astype(F32)).astype(BF16)
    comb_one[0] = ones_where(main)
    for k in range(3):
        here = (spot >> 2) == k
        sel_fold[:, k * TOK : (k + 1) * TOK] = ones_where(fold & here)
        w_here = jnp.where(here, fold_w, 0.0)
        comb_hi[1 + k] = w_here.astype(BF16)
        comb_lo[1 + k] = (w_here - w_here.astype(BF16).astype(F32)).astype(BF16)
        comb_one[1 + k] = ones_where(fold & here)
    main_scale = jnp.sum(main_w, 1, keepdims=True)
    fold_scale = jnp.sum(jnp.where((spot >> 2) < 3, fold_w, 0.0), 1, keepdims=True)

    start = pl.multiple_of(c * WIDE, WIDE)
    for a, source in enumerate((tok, og)):
        loads[a].wait()
        feats = source[pl.ds(start, WIDE), :]
        whole = dg(sel_main[...], feats, 1, 1)
        folded = jnp.zeros((256, GROUP), F32)
        for k in range(3):
            folded += dg(
                sel_fold[:, k * TOK : (k + 1) * TOK], feats[k * GROUP : (k + 1) * GROUP, :], 1, 1
            )
        if a == 1:
            whole = main_scale * whole
            folded = fold_scale * folded
        send_slab[a, :, 0:WIDE] = whole.astype(BF16)
        send_slab[a, :, WIDE:MSG] = folded.astype(BF16)

    pl.semaphore_wait(barrier, 30)

    def dispatch(a, i):
        return pltpu.make_async_remote_copy(
            src_ref=send_slab.at[a, slab_rows(peer(i))],
            dst_ref=cat.at[a, 0, c, slab_rows(me)],
            send_sem=xy_s.at[a, i], recv_sem=xy_r.at[a, i],
            device_id=(d, peer(i)), device_id_type=MESH,
        )

    def arrive(a, i):
        return pltpu.make_async_remote_copy(
            src_ref=send_slab.at[a, slab_rows(peer(i))],
            dst_ref=cat.at[a, 0, c, slab_rows(origin(i))],
            send_sem=xy_s.at[a, i], recv_sem=xy_r.at[a, i],
            device_id=(d, peer(i)), device_id_type=MESH,
        )

    def along_z(a, s):
        side = 1 - 2 * (s // 8)
        return pltpu.make_async_remote_copy(
            src_ref=cat.at[a, 0, c, slab_rows(s)],
            dst_ref=cat.at[a, 1, c, slab_rows(s)],
            send_sem=zf_s.at[a, s], recv_sem=zf_r.at[a, s],
            device_id=(lax.rem(z + side + 8, 8) * 2 + c, me), device_id_type=MESH,
        )

    def to_sibling(a, o, s):
        return pltpu.make_async_remote_copy(
            src_ref=cat.at[a, o, c, slab_rows(s)],
            dst_ref=cat.at[a, o, c, slab_rows(s)],
            send_sem=cf_s.at[a, o, s], recv_sem=cf_r.at[a, o, s],
            device_id=sib, device_id_type=MESH,
        )

    def from_sibling(a, o, s):
        return pltpu.make_async_remote_copy(
            src_ref=cat.at[a, o, c, slab_rows(s)],
            dst_ref=cat.at[a, o, 1 - c, slab_rows(s)],
            send_sem=cf_s.at[a, o, s], recv_sem=cf_r.at[a, o, s],
            device_id=sib, device_id_type=MESH,
        )

    def loop(lo, hi, body):
        def step(i, carry):
            body(i)
            return carry

        lax.fori_loop(lo, hi, step, 0)

    for a in range(2):
        cat[a, 0, c, slab_rows(me), :] = send_slab[a, slab_rows(me), :]
        loop(1, 16, lambda i, a=a: dispatch(a, i).start())

    n = iota((PAIR, 256), 0)
    i = iota((PAIR, 256), 1)
    later = jnp.where(n >= ROWS, 1, 0)
    m = n - ROWS * later
    s = (m * 6554) >> 16
    q = m - RANKS * s + RANKS * later
    grp[0] = ones_where((i == s * SLAB + q) & (q < 16))
    for k in range(3):
        grp[1 + k] = ones_where((i == s * SLAB + 4 * k + q - 16) & (q >= 16))
    n = iota((256, PAIR), 1)
    i = iota((256, PAIR), 0)
    later = jnp.where(n >= ROWS, 1, 0)
    m = n - ROWS * later
    s = (m * 6554) >> 16
    q = m - RANKS * s + RANKS * later
    ungrp[0] = ones_where((i == s * SLAB + q) & (q < 16))
    for k in range(3):
        ungrp[1 + k] = ones_where((i == s * SLAB + 4 * k + q - 16) & (q >= 16))
    line = iota((8 * BROWS, WIDE), 0)
    block = (line * 683) >> 16
    inner = line - BROWS * block
    blksel[...] = ones_where((iota((8 * BROWS, WIDE), 1) == BLK * block + inner) & (inner < BLK))

    def first_hop(a, lo, hi):
        def body(i):
            @pl.when(i > 0)
            def _():
                arrive(a, i).wait_recv()

            along_z(a, origin(i)).start()
            to_sibling(a, 0, origin(i)).start()

        loop(lo, hi, body)

    def second_hop(a):
        def body(s):
            along_z(a, s).wait_recv()
            to_sibling(a, 1, s).start()

        loop(0, 16, body)

    def regroup(a, o):
        loop(0, 16, lambda s: from_sibling(a, o, s).wait_recv())
        for h in range(2):
            folded = cat[a, o, h, :, WIDE:MSG]
            for k in range(3):
                value = dg(grp[0], cat[a, o, h, :, k * GROUP : (k + 1) * GROUP], 1, 0)
                value += dg(grp[1 + k], folded, 1, 0)
                rows[a, o, :, h * WIDE + k * GROUP : h * WIDE + (k + 1) * GROUP] = value.astype(BF16)

    def expert_of(o, le):
        return 2 * (par + o - 2 * par * o) + le

    def of_expert(le):
        return pl.ds(pl.multiple_of(le * ROWS, ROWS), ROWS)

    mine = pl.multiple_of(c * HALF, HALF)
    other = pl.multiple_of((1 - c) * HALF, HALF)

    def to_core(a, o):
        return pltpu.make_async_remote_copy(
            src_ref=part.at[a, 1, o], dst_ref=crecv.at[a, o],
            send_sem=rc_s.at[a, o], recv_sem=rc_r.at[a, o],
            device_id=sib, device_id_type=MESH,
        )

    def forward(o):
        regroup(0, o)

        def body(le):
            e = expert_of(o, le)
            r = of_expert(le)
            xe = rows[0, o, r, 0:D]
            pg = dg(xe, wg[e, pl.ds(0, D), :], 1, 0)
            pu = dg(xe, wu[e, pl.ds(0, D), :], 1, 0) + 1.0
            sg = jax.nn.sigmoid(1.702 * pg)
            ac = pg * sg
            sig[o, r, :] = sg
            pre[o, r, :] = pg
            act[o, r, :] = ac
            upp[o, r, :] = pu
            hd = (ac * pu).astype(BF16)
            hid[o, r, :] = hd
            part[0, 0, o, r, :] = dg(hd, wd[e, pl.ds(mine, WIDE), :], 1, 1).astype(BF16)
            part[0, 1, o, r, :] = dg(hd, wd[e, pl.ds(other, WIDE), :], 1, 1).astype(BF16)

        loop(0, 2, body)
        to_core(0, o).start()

    def backward(o):
        regroup(1, o)

        def body(le):
            e = expert_of(o, le)
            r = of_expert(le)
            ge = rows[1, o, r, 0:D]
            hg = dg(ge, wd[e, pl.ds(0, D), :], 1, 0)
            sg, pg, ac, pu = sig[o, r, :], pre[o, r, :], act[o, r, :], upp[o, r, :]
            slope = sg + 1.702 * pg * sg * (1.0 - sg)
            gate = (hg * pu * slope).astype(BF16)
            upg = (hg * ac).astype(BF16)
            ggu[o, r, 0:HID] = gate
            ggu[o, r, HID : 2 * HID] = upg
            dot = jnp.sum(hid[o, r, :].astype(F32) * hg, 1, keepdims=True)
            own = dg(gate, wg[e, pl.ds(mine, WIDE), :], 1, 1)
            own += dg(upg, wu[e, pl.ds(mine, WIDE), :], 1, 1)
            part[1, 0, o, r, :] = jnp.where(iota((ROWS, WIDE), 1) == HALF, dot, own).astype(BF16)
            far = dg(gate, wg[e, pl.ds(other, WIDE), :], 1, 1)
            far += dg(upg, wu[e, pl.ds(other, WIDE), :], 1, 1)
            part[1, 1, o, r, :] = jnp.where(iota((ROWS, WIDE), 1) == HALF, 0.0, far).astype(BF16)

        loop(0, 2, body)
        to_core(1, o).start()

    def across(a, le):
        return pltpu.make_async_remote_copy(
            src_ref=zsend.at[a, le], dst_ref=zrecv.at[a, le],
            send_sem=rz_s.at[a, le], recv_sem=rz_r.at[a, le],
            device_id=up if le == 0 else down, device_id_type=MESH,
        )

    def reduce_far(a):
        to_core(a, 1).wait_recv()
        for le in range(2):
            r = pl.ds(le * ROWS, ROWS)
            total = part[a, 0, 1, r, :].astype(F32) + crecv[a, 1, r, :].astype(F32)
            zsend[a, le] = total.astype(BF16)
            across(a, le).start()

    def give_back(a, i):
        return pltpu.make_async_remote_copy(
            src_ref=slab.at[a, slab_rows(peer(i))],
            dst_ref=back.at[a, slab_rows(me)],
            send_sem=bk_s.at[a, i], recv_sem=bk_r.at[a, i],
            device_id=(d, peer(i)), device_id_type=MESH,
        )

    def got_back(a, i):
        return pltpu.make_async_remote_copy(
            src_ref=slab.at[a, slab_rows(peer(i))],
            dst_ref=back.at[a, slab_rows(origin(i))],
            send_sem=bk_s.at[a, i], recv_sem=bk_r.at[a, i],
            device_id=(d, peer(i)), device_id_type=MESH,
        )

    def reduce_near(a):
        to_core(a, 0).wait_recv()
        totals = []
        for le in range(2):
            across(a, le).wait_recv()
            r = pl.ds(le * ROWS, ROWS)
            total = part[a, 0, 0, r, :].astype(F32) + crecv[a, 0, r, :].astype(F32)
            totals.append((total + zrecv[a, le].astype(F32)).astype(BF16))
        both = jnp.concatenate(totals, 0)
        slab[a, :, 0:WIDE] = dg(ungrp[0], both, 1, 0).astype(BF16)
        folded = jnp.zeros((256, GROUP), F32)
        for k in range(3):
            folded += dg(ungrp[1 + k], both[:, k * GROUP : (k + 1) * GROUP], 1, 0)
        slab[a, :, WIDE:MSG] = folded.astype(BF16)
        back[a, slab_rows(me), :] = slab[a, slab_rows(me), :]
        loop(1, 16, lambda i: give_back(a, i).start())

    def block_owner(k):
        return (4 * c + k // 2) * 2 + k % 2

    def hand_out(a, k):
        return pltpu.make_async_remote_copy(
            src_ref=blocks.at[a, k], dst_ref=frecv.at[a, z],
            send_sem=fb_s.at[a, k], recv_sem=fb_r.at[a, z],
            device_id=(block_owner(k), me), device_id_type=MESH,
        )

    def handed(a, zz):
        return pltpu.make_async_remote_copy(
            src_ref=blocks.at[a, 0], dst_ref=frecv.at[a, zz],
            send_sem=fb_s.at[a, 0], recv_sem=fb_r.at[a, zz],
            device_id=sib, device_id_type=MESH,
        )

    def tell(i):
        return pltpu.make_async_remote_copy(
            src_ref=dots.at[d], dst_ref=dots.at[d],
            send_sem=dt_s.at[i], recv_sem=dt_r.at[i],
            device_id=(lax.rem(d + i, 16), me), device_id_type=MESH,
        )

    def told(i):
        return pltpu.make_async_remote_copy(
            src_ref=dots.at[d], dst_ref=dots.at[lax.rem(d + 16 - i, 16)],
            send_sem=dt_s.at[i], recv_sem=dt_r.at[i],
            device_id=(lax.rem(d + i, 16), me), device_id_type=MESH,
        )

    def combine(a):
        loop(1, 16, lambda i: got_back(a, i).wait_recv())
        if a == 1:
            main_dot = back[1, :, HALF : HALF + 1].astype(F32)
            fold_dot = back[1, :, HALF + GROUP : HALF + GROUP + 1].astype(F32)
            main_dot = jnp.where(comb_one[0].astype(F32) > 0.5, main_dot, 0.0)
            fold_dot = jnp.where(comb_one[3].astype(F32) > 0.5, fold_dot, 0.0)
            lines = []
            for p in range(4):
                mine_p = jnp.where(ids[p : p + 1, :] == main_expert, main_dot, 0.0)
                mine_p += jnp.where(ids[p : p + 1, :] == fold_expert, fold_dot, 0.0)
                lines.append(jnp.sum(mine_p, 0, keepdims=True))
            dots[d] = jnp.concatenate(lines + [jnp.zeros((4, TOK), F32)], 0)
            loop(1, 16, lambda i: tell(i).start())
        tables = (comb_hi, comb_lo) if a == 0 else (comb_one,)
        pieces = []
        for k in range(3):
            value = jnp.zeros((TOK, GROUP), F32)
            for table in tables:
                value += dg(table[0], back[a, :, k * GROUP : (k + 1) * GROUP], 0, 0)
                value += dg(table[1 + k], back[a, :, WIDE:MSG], 0, 0)
            pieces.append(value.astype(BF16))
        total = dg(blksel[...], jnp.concatenate(pieces, 1), 1, 1).astype(BF16)
        for k in range(8):
            blocks[a, k] = total[k * BROWS : (k + 1) * BROWS, :]

        def body(k):
            @pl.when(block_owner(k) != d)
            def _():
                hand_out(a, k).start()

            @pl.when(block_owner(k) == d)
            def _():
                frecv[a, z] = blocks[a, k]

        loop(0, 8, body)

    def sender(zz):
        return zz * 2 + z // 4

    def finish(a, out_ref):
        def body(zz):
            @pl.when(sender(zz) != d)
            def _():
                handed(a, zz).wait_recv()

        loop(0, 8, body)
        total = frecv[a, 0].astype(F32)
        for zz in range(1, 8):
            total += frecv[a, zz].astype(F32)
        out_ref[...] = total[0:BLK, :].astype(BF16)

    def store(o, le, n):
        out = (gg_hbm, gu_hbm, gd_hbm)[n]
        e = expert_of(o, le)
        return pltpu.make_async_copy(grads.at[n, e], out.at[e], out_sem.at[n, e])

    def weight_grads(o):
        def body(le):
            e = expert_of(o, le)
            r = of_expert(le)
            both = dg(rows[0, o, r, 0:D], ggu[o, r, :], 0, 0)
            grads[0, e] = both[:, 0:HID].astype(BF16)
            grads[1, e] = both[:, HID : 2 * HID].astype(BF16)
            grads[2, e] = dg(rows[1, o, r, 0:D], hid[o, r, :], 0, 0).astype(BF16)
            for n in range(3):
                store(o, le, n).start()

        loop(0, 2, body)

    first_hop(0, 0, 16)
    second_hop(0)
    for load in loads[2:]:
        load.wait()
    first_hop(1, 0, 6)
    forward(0)
    first_hop(1, 6, 11)
    forward(1)
    first_hop(1, 11, 16)
    reduce_far(0)
    second_hop(1)
    backward(0)
    reduce_near(0)
    backward(1)
    reduce_far(1)
    weight_grads(0)
    reduce_near(1)
    combine(0)
    weight_grads(1)
    combine(1)
    finish(0, mixed_ref)
    finish(1, igrad_ref)
    loop(1, 16, lambda i: told(i).wait_recv())
    total = dots[0]
    for k in range(1, 16):
        total += dots[k]
    dot = total[0:4, :]
    rgrad_ref[...] = dot - weights * jnp.sum(dot, 0, keepdims=True)

    def sent(i):
        tell(i).wait_send()
        for a in range(2):
            dispatch(a, i).wait_send()
            give_back(a, i).wait_send()

    loop(1, 16, sent)

    def passed(s):
        for a in range(2):
            along_z(a, s).wait_send()
            for o in range(2):
                to_sibling(a, o, s).wait_send()

    loop(0, 16, passed)
    for a in range(2):
        for o in range(2):
            to_core(a, o).wait_send()
            across(a, o).wait_send()

        def out_block(k, a=a):
            @pl.when(block_owner(k) != d)
            def _():
                hand_out(a, k).wait_send()

        loop(0, 8, out_block)
    for o in range(2):
        for le in range(2):
            for n in range(3):
                store(o, le, n).wait()


def on_device(tokens, output_grad, router_logits, expert_ids, w_gate, w_up, w_down):
    anywhere = pl.BlockSpec(memory_space=pl.ANY)
    vmem = pl.BlockSpec(memory_space=pltpu.VMEM)
    dma = pltpu.SemaphoreType.DMA
    weight = jax.ShapeDtypeStruct((4, D, HID), BF16)
    block = jax.ShapeDtypeStruct((BLK, TOK), BF16)
    mixed, igrad, rgrad, gg, gu, gd = pl.pallas_call(
        kernel,
        out_shape=(block, block, jax.ShapeDtypeStruct((4, TOK), F32), weight, weight, weight),
        in_specs=[anywhere, anywhere, vmem, vmem, anywhere, anywhere, anywhere],
        out_specs=(vmem, vmem, vmem, anywhere, anywhere, anywhere),
        scratch_shapes=[
            pltpu.VMEM((PADDED, TOK), BF16),
            pltpu.VMEM((PADDED, TOK), BF16),
            pltpu.VMEM((4, D + WIDE - HALF, HID), BF16),
            pltpu.VMEM((4, D + WIDE - HALF, HID), BF16),
            pltpu.VMEM((4, D + WIDE - HALF, HID), BF16),
            pltpu.VMEM((2, 256, MSG), BF16),
            pltpu.VMEM((2, 2, 2, 256, MSG), BF16),
            pltpu.VMEM((2, 2, PAIR, PADDED), BF16),
            pltpu.VMEM((256, TOK), BF16),
            pltpu.VMEM((256, 3 * TOK), BF16),
            pltpu.VMEM((4, 256, TOK), BF16),
            pltpu.VMEM((4, 256, TOK), BF16),
            pltpu.VMEM((4, 256, TOK), BF16),
            pltpu.VMEM((4, PAIR, 256), BF16),
            pltpu.VMEM((4, 256, PAIR), BF16),
            pltpu.VMEM((8 * BROWS, WIDE), BF16),
            pltpu.VMEM((2, PAIR, HID), F32),
            pltpu.VMEM((2, PAIR, HID), F32),
            pltpu.VMEM((2, PAIR, HID), F32),
            pltpu.VMEM((2, PAIR, HID), F32),
            pltpu.VMEM((2, PAIR, HID), BF16),
            pltpu.VMEM((2, PAIR, 2 * HID), BF16),
            pltpu.VMEM((2, 2, 2, PAIR, WIDE), BF16),
            pltpu.VMEM((2, 2, PAIR, WIDE), BF16),
            pltpu.VMEM((2, 2, ROWS, WIDE), BF16),
            pltpu.VMEM((2, 2, ROWS, WIDE), BF16),
            pltpu.VMEM((2, 256, MSG), BF16),
            pltpu.VMEM((2, 256, MSG), BF16),
            pltpu.VMEM((2, 8, BROWS, TOK), BF16),
            pltpu.VMEM((2, 8, BROWS, TOK), BF16),
            pltpu.VMEM((16, 8, TOK), F32),
            pltpu.VMEM((3, 4, D, HID), BF16),
            dma((14,)),
            dma((2, 16)), dma((2, 16)),
            dma((2, 16)), dma((2, 16)),
            dma((2, 2, 16)), dma((2, 2, 16)),
            dma((2, 2)), dma((2, 2)),
            dma((2, 2)), dma((2, 2)),
            dma((2, 16)), dma((2, 16)),
            dma((2, 8)), dma((2, 8)),
            dma((16,)), dma((16,)),
            dma((3, 4)),
        ],
        compiler_params=pltpu.CompilerParams(
            collective_id=0, has_side_effects=True, vmem_limit_bytes=56 * 2**20
        ),
        cost_estimate=pl.CostEstimate(
            flops=2 * 9 * 640 * D * HID, bytes_accessed=9 * 10**6, transcendentals=640 * HID
        ),
        name="moe_layer",
    )(
        tokens.T, output_grad.T, router_logits.T, expert_ids.T,
        w_gate, w_up, jnp.swapaxes(w_down, 1, 2),
    )
    return mixed.T, igrad.T, rgrad.T, gg, gu, jnp.swapaxes(gd, 1, 2)


def solution(mesh):
    in_specs = (
        P("expert", None),
        P("expert", None),
        P("expert", None),
        P("expert", None),
        P("expert", None, "dp"),
        P("expert", None, "dp"),
        P("expert", "dp", None),
    )
    out_specs = (
        P("expert", "dp"),
        P("expert", "dp"),
        P("expert", None),
        P("expert", None, "dp"),
        P("expert", None, "dp"),
        P("expert", "dp", None),
    )
    return jax.shard_map(
        on_device, mesh=mesh, in_specs=in_specs, out_specs=out_specs, check_vma=False
    )
```

```python
import jax
import jax.numpy as jnp
import numpy as np
from jax import lax
from jax.experimental import pallas as pl
from jax.experimental.pallas import tpu as pltpu
from jax.sharding import PartitionSpec as P

MESH = pl.DeviceIdType.MESH
F32 = jnp.float32
BF16 = jnp.bfloat16

D = 1440
HALF = 720
WIDE = 768
PADDED = 1536
HID = 128
TOK = 128
RANKS = 10
SRC = 16
ROWS = SRC * RANKS
PAIR = 2 * ROWS
SLAB = 16
MSG = 1024
GROUP = 256
PART = 384
STEP = 352
BACK = 512
DOT_LANE = 376
ORDER = (1, 12, 3, 4, 2, 8, 5, 15, 7, 13, 6, 14, 9, 11, 10)
FIRST = int(np.int32(np.uint32(sum(i << (4 * j) for j, i in enumerate(ORDER[:8])))))
LAST = sum(i << (4 * j) for j, i in enumerate(ORDER[8:]))
BLK = 90
BROWS = 96


def dg(a, b, ca, cb):
    return lax.dot_general(a, b, (((ca,), (cb,)), ((), ())), preferred_element_type=F32)


def iota(shape, dim):
    return lax.broadcasted_iota(jnp.int32, shape, dim)


def ones_where(mask):
    return jnp.where(mask, 1.0, 0.0).astype(BF16)


def kernel(
    tok_hbm, og_hbm, logits_ref, ids_ref, wg_hbm, wu_hbm, wd_hbm,
    mixed_ref, igrad_ref, rgrad_ref, gg_hbm, gu_hbm, gd_hbm,
    tok, og, wgu, wd,
    send_slab, cat, rows, sel_main, sel_fold, comb_hi, comb_lo, comb_one,
    grp, ungrp, blksel,
    sig, pre, act, upp, hid, ggu, dotc,
    part, crecv, zsend, zrecv, slab, back, blocks, frecv, dots,
    grads,
    in_sem, xy_s, xy_r, zf_s, zf_r, cf_s, cf_r, rc_s, rc_r, rz_s, rz_r,
    bk_s, bk_r, fb_s, fb_r, dt_s, dt_r, out_sem,
):
    d = lax.axis_index("dp")
    me = lax.axis_index("expert")
    z, c = lax.div(d, 2), lax.rem(d, 2)
    x, y = lax.div(me, 4), lax.rem(me, 4)
    par = lax.rem(z, 2)
    sib = (z * 2 + 1 - c, me)
    up = (lax.rem(z + 1, 8) * 2 + c, me)
    down = (lax.rem(z + 7, 8) * 2 + c, me)

    def peer(i):
        return lax.rem(x + i // 4, 4) * 4 + lax.rem(y + i % 4, 4)

    def origin(i):
        return lax.rem(x + 4 - i // 4, 4) * 4 + lax.rem(y + 4 - i % 4, 4)

    def slab_rows(s):
        return pl.ds(pl.multiple_of(s * SLAB, SLAB), SLAB)

    barrier = pltpu.get_barrier_semaphore()

    def greet(i, carry):
        pl.semaphore_signal(barrier, inc=1, device_id=(d, peer(i)), device_id_type=MESH)
        pl.semaphore_signal(
            barrier, inc=1, device_id=(lax.rem(d + i, 16), me), device_id_type=MESH
        )
        return carry

    lax.fori_loop(1, 16, greet, 0)

    loads = [
        pltpu.make_async_copy(tok_hbm, tok.at[pl.ds(0, D)], in_sem.at[0]),
        pltpu.make_async_copy(og_hbm, og.at[pl.ds(0, D)], in_sem.at[1]),
    ]
    for e in range(4):
        for n, src, dst in (
            (2, wg_hbm, wgu.at[e, pl.ds(0, D), pl.ds(0, HID)]),
            (2, wu_hbm, wgu.at[e, pl.ds(0, D), pl.ds(HID, HID)]),
            (3, wd_hbm, wd.at[e, pl.ds(0, D)]),
        ):
            loads.append(pltpu.make_async_copy(src.at[e], dst, in_sem.at[n]))
    loads[0].start()
    loads[1].start()
    tok[pl.ds(D, PADDED - D), :] = jnp.zeros((PADDED - D, TOK), BF16)
    og[pl.ds(D, PADDED - D), :] = jnp.zeros((PADDED - D, TOK), BF16)

    lifted = jnp.exp(logits_ref[...])
    weights = lifted / jnp.sum(lifted, 0, keepdims=True)
    ids = ids_ref[...]
    row = iota((256, TOK), 0)
    spot = row & 15
    earlier = ones_where(iota((TOK, TOK), 0) < iota((TOK, TOK), 1))

    def select(expert, rank):
        named = jnp.zeros((256, TOK), F32)
        weigh = jnp.zeros((256, TOK), F32)
        for p in range(4):
            same = ids[p : p + 1, :] == expert
            named = jnp.where(same, 1.0, named)
            weigh = jnp.where(same, weights[p : p + 1, :], weigh)
        before = dg(named.astype(BF16), earlier, 1, 0)
        chosen = (before == rank.astype(F32)) & (named > 0.5)
        return chosen, jnp.where(chosen, weigh, 0.0)

    second = jnp.where(spot >= RANKS, 1, 0)
    base = 4 * (row >> 4) + 2 * par
    main_expert = base + second
    fold_expert = base + 1
    main, main_w = select(main_expert, spot - RANKS * second)
    fold, fold_w = select(fold_expert, 6 + (spot & 3))
    sel_main[...] = ones_where(main)
    for k in range(3):
        sel_fold[:, k * TOK : (k + 1) * TOK] = ones_where(fold & ((spot >> 2) == k))
    start = pl.multiple_of(c * WIDE, WIDE)

    def gather(a, source):
        loads[a].wait()
        whole = dg(sel_main[...], source[pl.ds(start, WIDE), :], 1, 1)
        folded = jnp.zeros((256, GROUP), F32)
        for k in range(3):
            feats = source[pl.ds(pl.multiple_of(start + k * GROUP, GROUP), GROUP), :]
            folded += dg(sel_fold[:, k * TOK : (k + 1) * TOK], feats, 1, 1)
        if a == 1:
            whole = jnp.sum(main_w, 1, keepdims=True) * whole
            some = jnp.where((spot >> 2) < 3, fold_w, 0.0)
            folded = jnp.sum(some, 1, keepdims=True) * folded
        send_slab[a, :, 0:WIDE] = whole.astype(BF16)
        send_slab[a, :, WIDE:MSG] = folded.astype(BF16)

    def dispatch(a, i):
        return pltpu.make_async_remote_copy(
            src_ref=send_slab.at[a, slab_rows(peer(i))],
            dst_ref=cat.at[a, 0, c, slab_rows(me)],
            send_sem=xy_s.at[a], recv_sem=xy_r.at[a, i],
            device_id=(d, peer(i)), device_id_type=MESH,
        )

    def arrive(a, i):
        return pltpu.make_async_remote_copy(
            src_ref=send_slab.at[a, slab_rows(peer(i))],
            dst_ref=cat.at[a, 0, c, slab_rows(origin(i))],
            send_sem=xy_s.at[a], recv_sem=xy_r.at[a, i],
            device_id=(d, peer(i)), device_id_type=MESH,
        )

    def along_z(a, s):
        side = s // 8
        return pltpu.make_async_remote_copy(
            src_ref=cat.at[a, 0, c, slab_rows(s)],
            dst_ref=cat.at[a, 1, c, slab_rows(s)],
            send_sem=zf_s.at[a], recv_sem=zf_r.at[a, side],
            device_id=(lax.rem(z + 1 - 2 * side + 8, 8) * 2 + c, me), device_id_type=MESH,
        )

    def along_z_all(a, side):
        eight = pl.ds(8 * SLAB * side, 8 * SLAB)
        return pltpu.make_async_remote_copy(
            src_ref=cat.at[a, 0, c, eight], dst_ref=cat.at[a, 1, c, eight],
            send_sem=zf_s.at[a], recv_sem=zf_r.at[a, side],
            device_id=down if side else up, device_id_type=MESH,
        )

    def to_sibling(a, o, s, count=1):
        some = pl.ds(pl.multiple_of(s * SLAB, SLAB), count * SLAB)
        return pltpu.make_async_remote_copy(
            src_ref=cat.at[a, o, c, some], dst_ref=cat.at[a, o, c, some],
            send_sem=cf_s.at[a, o], recv_sem=cf_r.at[a, o],
            device_id=sib, device_id_type=MESH,
        )

    def from_sibling(a, o):
        return pltpu.make_async_remote_copy(
            src_ref=cat.at[a, o, c], dst_ref=cat.at[a, o, 1 - c],
            send_sem=cf_s.at[a, o], recv_sem=cf_r.at[a, o],
            device_id=sib, device_id_type=MESH,
        )

    def loop(lo, hi, body):
        def step(i, carry):
            body(i)
            return carry

        lax.fori_loop(lo, hi, step, 0)

    def turn(j):
        return (jnp.where(j < 8, FIRST, LAST) >> (4 * lax.rem(j, 8))) & 15

    gather(0, tok)
    pl.semaphore_wait(barrier, 30)
    loop(0, 15, lambda j: dispatch(0, turn(j)).start())
    cat[0, 0, c, slab_rows(me), :] = send_slab[0, slab_rows(me), :]
    along_z(0, me).start()
    to_sibling(0, 0, me).start()
    for load in loads[2:]:
        load.start()
    gather(1, og)
    cat[1, 0, c, slab_rows(me), :] = send_slab[1, slab_rows(me), :]

    for e in range(4):
        wgu[e, pl.ds(D, WIDE - HALF), :] = jnp.zeros((WIDE - HALF, 2 * HID), BF16)
        wd[e, pl.ds(D, WIDE - HALF), :] = jnp.zeros((WIDE - HALF, HID), BF16)
    comb_hi[0] = main_w.astype(BF16)
    comb_lo[0] = (main_w - main_w.astype(BF16).astype(F32)).astype(BF16)
    comb_one[0] = sel_main[...]
    for k in range(3):
        here = (spot >> 2) == k
        w_here = jnp.where(here, fold_w, 0.0)
        comb_hi[1 + k] = w_here.astype(BF16)
        comb_lo[1 + k] = (w_here - w_here.astype(BF16).astype(F32)).astype(BF16)
        comb_one[1 + k] = sel_fold[:, k * TOK : (k + 1) * TOK]

    n = iota((PAIR, 256), 0)
    i = iota((PAIR, 256), 1)
    later = jnp.where(n >= ROWS, 1, 0)
    m = n - ROWS * later
    s = (m * 6554) >> 16
    q = m - RANKS * s + RANKS * later
    grp[0] = ones_where((i == s * SLAB + q) & (q < 16))
    for k in range(3):
        grp[1 + k] = ones_where((i == s * SLAB + 4 * k + q - 16) & (q >= 16))
    n = iota((256, PAIR), 1)
    i = iota((256, PAIR), 0)
    later = jnp.where(n >= ROWS, 1, 0)
    m = n - ROWS * later
    s = (m * 6554) >> 16
    q = m - RANKS * s + RANKS * later
    ungrp[0] = ones_where((i == s * SLAB + q) & (q < 16))
    for k in range(3):
        ungrp[1 + k] = ones_where((i == s * SLAB + 4 * k + q - 16) & (q >= 16))
    line = iota((4 * BROWS, PART), 0)
    block = (line * 683) >> 16
    inner = line - BROWS * block
    place = BLK * block + inner
    for f in range(2):
        blksel[f] = ones_where((iota((4 * BROWS, PART), 1) == place + 8 * f) & (inner < BLK))

    def first_hop(a, lo, hi):
        def body(j):
            i = turn(j)
            arrive(a, i).wait_recv()

            along_z(a, origin(i)).start()
            to_sibling(a, 0, origin(i)).start()
            if a == 0:
                dispatch(1, i).start()

        loop(lo, hi, body)

    def second_hop(a):
        for side in range(2):
            along_z_all(a, side).wait_recv()
            to_sibling(a, 1, 8 * side, 8).start()

    def regroup(a, o):
        from_sibling(a, o).wait_recv()
        for h in range(2):
            folded = cat[a, o, h, :, WIDE:MSG]
            for k in range(3):
                value = dg(grp[0], cat[a, o, h, :, k * GROUP : (k + 1) * GROUP], 1, 0)
                value += dg(grp[1 + k], folded, 1, 0)
                rows[a, o, :, h * WIDE + k * GROUP : h * WIDE + (k + 1) * GROUP] = value.astype(BF16)

    def expert_of(o, le):
        return 2 * (par + o - 2 * par * o) + le

    def of_expert(le):
        return pl.ds(pl.multiple_of(le * ROWS, ROWS), ROWS)

    def feats(far, f):
        side = 1 - c if far else c
        return pl.ds(pl.multiple_of(side * HALF + f * STEP, 16), PART)

    def to_core(a, f, o):
        return pltpu.make_async_remote_copy(
            src_ref=part.at[a, 1, f, o], dst_ref=crecv.at[a, f, o],
            send_sem=rc_s.at[a], recv_sem=rc_r.at[a, f, o],
            device_id=sib, device_id_type=MESH,
        )

    def forward(o):
        regroup(0, o)

        def body(le):
            e = expert_of(o, le)
            r = of_expert(le)
            xe = rows[0, o, r, 0:D]
            both = dg(xe, wgu[e, pl.ds(0, D), :], 1, 0)
            pg = both[:, 0:HID]
            pu = both[:, HID : 2 * HID] + 1.0
            sg = jax.nn.sigmoid(1.702 * pg)
            ac = pg * sg
            sig[o, r, :] = sg
            pre[o, r, :] = pg
            act[o, r, :] = ac
            upp[o, r, :] = pu
            hid[o, r, :] = (ac * pu).astype(BF16)

        loop(0, 2, body)

    def outputs(o, f):
        def body(le):
            e = expert_of(o, le)
            r = of_expert(le)
            for far in range(2):
                value = dg(hid[o, r, :], wd[e, feats(far, f), :], 1, 1)
                part[0, far, f, o, r, :] = value.astype(BF16)

        loop(0, 2, body)
        to_core(0, f, o).start()

    def backward(o):
        regroup(1, o)

        def body(le):
            e = expert_of(o, le)
            r = of_expert(le)
            ge = rows[1, o, r, 0:D]
            hg = dg(ge, wd[e, pl.ds(0, D), :], 1, 0)
            sg, pg, ac, pu = sig[o, r, :], pre[o, r, :], act[o, r, :], upp[o, r, :]
            slope = sg + 1.702 * pg * sg * (1.0 - sg)
            ggu[o, r, 0:HID] = (hg * pu * slope).astype(BF16)
            ggu[o, r, HID : 2 * HID] = (hg * ac).astype(BF16)
            dot = jnp.sum(hid[o, r, :].astype(F32) * hg, 1, keepdims=True)
            dotc[o, r, :] = jnp.broadcast_to(dot, (ROWS, HID))

        loop(0, 2, body)

    def inputs(o, f):
        def body(le):
            e = expert_of(o, le)
            r = of_expert(le)
            for far in range(2):
                value = dg(ggu[o, r, :], wgu[e, feats(far, f), :], 1, 1)
                if f == 1:
                    dot = dotc[o, r, 0:1] if far == 0 else 0.0
                    value = jnp.where(iota((ROWS, PART), 1) == DOT_LANE, dot, value)
                part[1, far, f, o, r, :] = value.astype(BF16)

        loop(0, 2, body)
        to_core(1, f, o).start()

    def across(a, f, le):
        return pltpu.make_async_remote_copy(
            src_ref=zsend.at[a, f, le], dst_ref=zrecv.at[a, f, le],
            send_sem=rz_s.at[a], recv_sem=rz_r.at[a, f],
            device_id=up if le == 0 else down, device_id_type=MESH,
        )

    def reduce_far(a, f):
        to_core(a, f, 1).wait_recv()
        for le in range(2):
            r = pl.ds(le * ROWS, ROWS)
            total = part[a, 0, f, 1, r, :].astype(F32) + crecv[a, f, 1, r, :].astype(F32)
            zsend[a, f, le] = total.astype(BF16)
            across(a, f, le).start()

    def give_back(a, f, i):
        return pltpu.make_async_remote_copy(
            src_ref=slab.at[a, f, slab_rows(peer(i))],
            dst_ref=back.at[a, f, slab_rows(me)],
            send_sem=bk_s.at[a, f], recv_sem=bk_r.at[a, f],
            device_id=(d, peer(i)), device_id_type=MESH,
        )

    def all_back(a, f):
        fifteen = pl.ds(0, 15 * SLAB)
        return pltpu.make_async_remote_copy(
            src_ref=slab.at[a, f, fifteen], dst_ref=back.at[a, f, fifteen],
            send_sem=bk_s.at[a, f], recv_sem=bk_r.at[a, f],
            device_id=sib, device_id_type=MESH,
        )

    def reduce_near(a, f):
        to_core(a, f, 0).wait_recv()
        totals = []
        pltpu.make_async_remote_copy(
            src_ref=zsend.at[a, f], dst_ref=zrecv.at[a, f],
            send_sem=rz_s.at[a], recv_sem=rz_r.at[a, f],
            device_id=up, device_id_type=MESH,
        ).wait_recv()
        for le in range(2):
            r = pl.ds(le * ROWS, ROWS)
            total = part[a, 0, f, 0, r, :].astype(F32) + crecv[a, f, 0, r, :].astype(F32)
            totals.append((total + zrecv[a, f, le].astype(F32)).astype(BF16))
        both = jnp.concatenate(totals, 0)
        slab[a, f, :, 0:PART] = dg(ungrp[0], both, 1, 0).astype(BF16)
        folded = jnp.zeros((256, TOK), F32)
        for k in range(3):
            folded += dg(ungrp[1 + k], both[:, k * TOK : (k + 1) * TOK], 1, 0)
        slab[a, f, :, PART:BACK] = folded.astype(BF16)
        back[a, f, slab_rows(me), :] = slab[a, f, slab_rows(me), :]
        loop(1, 16, lambda i: give_back(a, f, i).start())

    def block_owner(k):
        return (4 * c + k // 2) * 2 + k % 2

    def hand_out(a, k):
        return pltpu.make_async_remote_copy(
            src_ref=blocks.at[a, k], dst_ref=frecv.at[a, z],
            send_sem=fb_s.at[a], recv_sem=fb_r.at[a],
            device_id=(block_owner(k), me), device_id_type=MESH,
        )

    def handed(a, count):
        return pltpu.make_async_remote_copy(
            src_ref=blocks.at[a, pl.ds(0, count)], dst_ref=frecv.at[a, pl.ds(0, count)],
            send_sem=fb_s.at[a], recv_sem=fb_r.at[a],
            device_id=sib, device_id_type=MESH,
        )

    def tell(i):
        return pltpu.make_async_remote_copy(
            src_ref=dots.at[d], dst_ref=dots.at[d],
            send_sem=dt_s, recv_sem=dt_r,
            device_id=(lax.rem(d + i, 16), me), device_id_type=MESH,
        )

    def told():
        return pltpu.make_async_remote_copy(
            src_ref=dots.at[pl.ds(0, 15)], dst_ref=dots.at[pl.ds(0, 15)],
            send_sem=dt_s, recv_sem=dt_r,
            device_id=sib, device_id_type=MESH,
        )

    def combine(a, f):
        all_back(a, f).wait_recv()
        if a == 1 and f == 1:
            main_dot = back[1, 1, :, DOT_LANE : DOT_LANE + 1].astype(F32)
            lane = DOT_LANE + TOK
            fold_dot = back[1, 1, :, lane : lane + 1].astype(F32)
            main_dot = jnp.where(comb_one[0].astype(F32) > 0.5, main_dot, 0.0)
            fold_dot = jnp.where(comb_one[3].astype(F32) > 0.5, fold_dot, 0.0)
            lines = []
            for p in range(4):
                mine_p = jnp.where(ids[p : p + 1, :] == main_expert, main_dot, 0.0)
                mine_p += jnp.where(ids[p : p + 1, :] == fold_expert, fold_dot, 0.0)
                lines.append(jnp.sum(mine_p, 0, keepdims=True))
            dots[d] = jnp.concatenate(lines + [jnp.zeros((4, TOK), F32)], 0)
            loop(1, 16, lambda i: tell(i).start())
        tables = (comb_hi, comb_lo) if a == 0 else (comb_one,)
        value = jnp.zeros((TOK, PART), F32)
        for table in tables:
            value += dg(table[0], back[a, f, :, 0:PART], 0, 0)
            value += jnp.concatenate(
                [dg(table[1 + k], back[a, f, :, PART:BACK], 0, 0) for k in range(3)], 1
            )
        total = dg(blksel[f], value.astype(BF16), 1, 1).astype(BF16)
        for k in range(4):
            blocks[a, 4 * f + k] = total[k * BROWS : (k + 1) * BROWS, :]

        def body(k):
            @pl.when(block_owner(k) != d)
            def _():
                hand_out(a, k).start()

            @pl.when(block_owner(k) == d)
            def _():
                frecv[a, z] = blocks[a, k]

        loop(4 * f, 4 * f + 4, body)

    inside = lax.div(z, 4) == c

    def finish(a, out_ref):
        @pl.when(inside)
        def _():
            handed(a, 7).wait_recv()

        @pl.when(jnp.logical_not(inside))
        def _():
            handed(a, 8).wait_recv()

        total = frecv[a, 0].astype(F32)
        for zz in range(1, 8):
            total += frecv[a, zz].astype(F32)
        out_ref[...] = total[0:BLK, :].astype(BF16)

    def store(o, le, n):
        out = (gg_hbm, gu_hbm, gd_hbm)[n]
        e = expert_of(o, le)
        return pltpu.make_async_copy(grads.at[n, e], out.at[e], out_sem.at[n])

    def weight_grads(o):
        def body(le):
            e = expert_of(o, le)
            r = of_expert(le)
            both = dg(rows[0, o, r, 0:D], ggu[o, r, :], 0, 0)
            grads[0, e] = both[:, 0:HID].astype(BF16)
            grads[1, e] = both[:, HID : 2 * HID].astype(BF16)
            grads[2, e] = dg(rows[1, o, r, 0:D], hid[o, r, :], 0, 0).astype(BF16)
            for n in range(3):
                store(o, le, n).start()

        loop(0, 2, body)

    first_hop(0, 0, 15)
    along_z(1, me).start()
    to_sibling(1, 0, me).start()
    for n, w in ((2, wgu), (3, wd)):
        all_rows = w.at[:, pl.ds(0, D)]
        pltpu.make_async_copy(all_rows, all_rows, in_sem.at[n]).wait()
    forward(0)
    outputs(0, 0)
    outputs(0, 1)
    second_hop(0)
    first_hop(1, 0, 8)
    forward(1)
    outputs(1, 0)
    outputs(1, 1)
    first_hop(1, 8, 15)
    reduce_far(0, 0)
    reduce_far(0, 1)
    backward(0)
    second_hop(1)
    reduce_near(0, 0)
    reduce_near(0, 1)
    backward(1)
    for f in range(2):
        inputs(1, f)
        inputs(0, f)
    reduce_far(1, 0)
    reduce_far(1, 1)
    weight_grads(0)
    reduce_near(1, 0)
    reduce_near(1, 1)
    combine(0, 0)
    combine(0, 1)
    weight_grads(1)
    combine(1, 0)
    combine(1, 1)
    finish(0, mixed_ref)
    finish(1, igrad_ref)
    told().wait_recv()
    total = dots[0]
    for k in range(1, 16):
        total += dots[k]
    dot = total[0:4, :]
    rgrad_ref[...] = dot - weights * jnp.sum(dot, 0, keepdims=True)

    told().wait_send()
    for a in range(2):
        fifteen = pl.ds(0, 15 * SLAB)
        pltpu.make_async_remote_copy(
            src_ref=send_slab.at[a, fifteen], dst_ref=cat.at[a, 0, c, fifteen],
            send_sem=xy_s.at[a], recv_sem=xy_r.at[a, 0],
            device_id=sib, device_id_type=MESH,
        ).wait_send()
        pltpu.make_async_remote_copy(
            src_ref=cat.at[a, 0, c], dst_ref=cat.at[a, 1, c],
            send_sem=zf_s.at[a], recv_sem=zf_r.at[a, 0],
            device_id=sib, device_id_type=MESH,
        ).wait_send()
        pltpu.make_async_remote_copy(
            src_ref=part.at[a, 1], dst_ref=crecv.at[a],
            send_sem=rc_s.at[a], recv_sem=rc_r.at[a, 0, 0],
            device_id=sib, device_id_type=MESH,
        ).wait_send()
        pltpu.make_async_remote_copy(
            src_ref=zsend.at[a], dst_ref=zrecv.at[a],
            send_sem=rz_s.at[a], recv_sem=rz_r.at[a, 0],
            device_id=sib, device_id_type=MESH,
        ).wait_send()
        for f in range(2):
            from_sibling(a, f).wait_send()
            all_back(a, f).wait_send()

        @pl.when(inside)
        def _():
            handed(a, 7).wait_send()

        @pl.when(jnp.logical_not(inside))
        def _():
            handed(a, 8).wait_send()

    for n, out in enumerate((gg_hbm, gu_hbm, gd_hbm)):
        pltpu.make_async_copy(grads.at[n], out, out_sem.at[n]).wait()


def deliver(mixed_in, igrad_in, rgrad_in, gg_in, gu_in, gd_in, *outs):
    for src, dst in zip((mixed_in, igrad_in, rgrad_in, gg_in, gu_in, gd_in), outs):
        dst[...] = src[...]


def on_device(tokens, output_grad, router_logits, expert_ids, w_gate, w_up, w_down):
    anywhere = pl.BlockSpec(memory_space=pl.ANY)
    vmem = pl.BlockSpec(memory_space=pltpu.VMEM)
    dma = pltpu.SemaphoreType.DMA
    weight = jax.ShapeDtypeStruct((4, D, HID), BF16)
    block = jax.ShapeDtypeStruct((BLK, TOK), BF16)
    mixed, igrad, rgrad, gg, gu, gd = pl.pallas_call(
        kernel,
        out_shape=(block, block, jax.ShapeDtypeStruct((4, TOK), F32), weight, weight, weight),
        in_specs=[anywhere, anywhere, vmem, vmem, anywhere, anywhere, anywhere],
        out_specs=(vmem, vmem, vmem, anywhere, anywhere, anywhere),
        scratch_shapes=[
            pltpu.VMEM((PADDED, TOK), BF16),
            pltpu.VMEM((PADDED, TOK), BF16),
            pltpu.VMEM((4, D + WIDE - HALF, 2 * HID), BF16),
            pltpu.VMEM((4, D + WIDE - HALF, HID), BF16),
            pltpu.VMEM((2, 256, MSG), BF16),
            pltpu.VMEM((2, 2, 2, 256, MSG), BF16),
            pltpu.VMEM((2, 2, PAIR, PADDED), BF16),
            pltpu.VMEM((256, TOK), BF16),
            pltpu.VMEM((256, 3 * TOK), BF16),
            pltpu.VMEM((4, 256, TOK), BF16),
            pltpu.VMEM((4, 256, TOK), BF16),
            pltpu.VMEM((4, 256, TOK), BF16),
            pltpu.VMEM((4, PAIR, 256), BF16),
            pltpu.VMEM((4, 256, PAIR), BF16),
            pltpu.VMEM((2, 4 * BROWS, PART), BF16),
            pltpu.VMEM((2, PAIR, HID), F32),
            pltpu.VMEM((2, PAIR, HID), F32),
            pltpu.VMEM((2, PAIR, HID), F32),
            pltpu.VMEM((2, PAIR, HID), F32),
            pltpu.VMEM((2, PAIR, HID), BF16),
            pltpu.VMEM((2, PAIR, 2 * HID), BF16),
            pltpu.VMEM((2, PAIR, HID), F32),
            pltpu.VMEM((2, 2, 2, 2, PAIR, PART), BF16),
            pltpu.VMEM((2, 2, 2, PAIR, PART), BF16),
            pltpu.VMEM((2, 2, 2, ROWS, PART), BF16),
            pltpu.VMEM((2, 2, 2, ROWS, PART), BF16),
            pltpu.VMEM((2, 2, 256, BACK), BF16),
            pltpu.VMEM((2, 2, 256, BACK), BF16),
            pltpu.VMEM((2, 8, BROWS, TOK), BF16),
            pltpu.VMEM((2, 8, BROWS, TOK), BF16),
            pltpu.VMEM((16, 8, TOK), F32),
            pltpu.VMEM((3, 4, D, HID), BF16),
            dma((4,)),
            dma((2,)), dma((2, 16)),
            dma((2,)), dma((2, 2)),
            dma((2, 2)), dma((2, 2)),
            dma((2,)), dma((2, 2, 2)),
            dma((2,)), dma((2, 2)),
            dma((2, 2)), dma((2, 2)),
            dma((2,)), dma((2,)),
            dma(()), dma(()),
            dma((3,)),
        ],
        compiler_params=pltpu.CompilerParams(
            collective_id=0, has_side_effects=True, vmem_limit_bytes=58 * 2**20
        ),
        cost_estimate=pl.CostEstimate(
            flops=2 * 9 * 640 * D * HID, bytes_accessed=9 * 10**6, transcendentals=640 * HID
        ),
        name="moe_layer",
    )(
        tokens.T, output_grad.T, router_logits.T, expert_ids.T,
        w_gate, w_up, jnp.swapaxes(w_down, 1, 2),
    )
    small = pl.BlockSpec((BLK, TOK), lambda e: (0, 0))
    tiny = pl.BlockSpec((4, TOK), lambda e: (0, 0))
    large = pl.BlockSpec((1, D, HID), lambda e: (e, 0, 0))
    mixed, igrad, rgrad, gg, gu, gd = pl.pallas_call(
        deliver,
        grid=(4,),
        out_shape=(block, block, jax.ShapeDtypeStruct((4, TOK), F32), weight, weight, weight),
        in_specs=[small, small, tiny, large, large, large],
        out_specs=(small, small, tiny, large, large, large),
        cost_estimate=pl.CostEstimate(flops=0, bytes_accessed=9 * 10**6, transcendentals=0),
        name="deliver",
    )(mixed, igrad, rgrad, gg, gu, gd)
    return mixed.T, igrad.T, rgrad.T, gg, gu, jnp.swapaxes(gd, 1, 2)


def solution(mesh):
    in_specs = (
        P("expert", None),
        P("expert", None),
        P("expert", None),
        P("expert", None),
        P("expert", None, "dp"),
        P("expert", None, "dp"),
        P("expert", "dp", None),
    )
    out_specs = (
        P("expert", "dp"),
        P("expert", "dp"),
        P("expert", None),
        P("expert", None, "dp"),
        P("expert", None, "dp"),
        P("expert", "dp", None),
    )
    return jax.shard_map(
        on_device, mesh=mesh, in_specs=in_specs, out_specs=out_specs, check_vma=False
    )
```

```python
import jax
import jax.numpy as jnp
import numpy as np
from jax import lax
from jax.experimental import pallas as pl
from jax.experimental.pallas import tpu as pltpu
from jax.sharding import PartitionSpec as P

MESH = pl.DeviceIdType.MESH
F32 = jnp.float32
BF16 = jnp.bfloat16

D = 1440
HALF = 720
WIDE = 768
PADDED = 1536
HID = 128
TOK = 128
RANKS = 10
SRC = 16
ROWS = SRC * RANKS
PAIR = 2 * ROWS
SLAB = 16
MSG = 1024
GROUP = 256
PART = 384
STEP = 352
BACK = 512
DOT_LANE = 376
ORDER = (1, 12, 3, 4, 2, 8, 5, 15, 7, 13, 6, 14, 9, 11, 10)
FIRST = int(np.int32(np.uint32(sum(i << (4 * j) for j, i in enumerate(ORDER[:8])))))
LAST = sum(i << (4 * j) for j, i in enumerate(ORDER[8:]))
BLK = 90
BROWS = 96


def dg(a, b, ca, cb):
    return lax.dot_general(a, b, (((ca,), (cb,)), ((), ())), preferred_element_type=F32)


def iota(shape, dim):
    return lax.broadcasted_iota(jnp.int32, shape, dim)


def ones_where(mask):
    return jnp.where(mask, 1.0, 0.0).astype(BF16)


def kernel(
    tok_hbm, og_hbm, logits_ref, ids_ref, wg_hbm, wu_hbm, wd_hbm,
    mixed_ref, igrad_ref, rgrad_ref, gg_hbm, gu_hbm, gd_hbm,
    tok, og, wgu, wd,
    send_slab, cat, rows, sel_main, sel_fold, comb_hi, comb_lo, comb_one,
    grp, ungrp, blksel,
    sig, pre, act, upp, hid, ggu, dotc,
    part, crecv, zsend, zrecv, slab, back, blocks, frecv, dots,
    grads,
    in_sem, xy_s, xy_r, zf_s, zf_r, cf_s, cf_r, rc_s, rc_r, rz_s, rz_r,
    bk_s, bk_r, fb_s, fb_r, dt_s, dt_r, out_sem,
):
    d = lax.axis_index("dp")
    me = lax.axis_index("expert")
    z, c = lax.div(d, 2), lax.rem(d, 2)
    x, y = lax.div(me, 4), lax.rem(me, 4)
    par = lax.rem(z, 2)
    sib = (z * 2 + 1 - c, me)
    up = (lax.rem(z + 1, 8) * 2 + c, me)
    down = (lax.rem(z + 7, 8) * 2 + c, me)

    def peer(i):
        return lax.rem(x + i // 4, 4) * 4 + lax.rem(y + i % 4, 4)

    def origin(i):
        return lax.rem(x + 4 - i // 4, 4) * 4 + lax.rem(y + 4 - i % 4, 4)

    def slab_rows(s):
        return pl.ds(pl.multiple_of(s * SLAB, SLAB), SLAB)

    barrier = pltpu.get_barrier_semaphore()

    def greet(i, carry):
        pl.semaphore_signal(barrier, inc=1, device_id=(d, peer(i)), device_id_type=MESH)
        pl.semaphore_signal(
            barrier, inc=1, device_id=(lax.rem(d + i, 16), me), device_id_type=MESH
        )
        return carry

    lax.fori_loop(1, 16, greet, 0)

    loads = [
        pltpu.make_async_copy(tok_hbm, tok.at[pl.ds(0, D)], in_sem.at[0]),
        pltpu.make_async_copy(og_hbm, og.at[pl.ds(0, D)], in_sem.at[1]),
    ]
    for e in range(4):
        for n, src, dst in (
            (2, wg_hbm, wgu.at[e, pl.ds(0, D), pl.ds(0, HID)]),
            (2, wu_hbm, wgu.at[e, pl.ds(0, D), pl.ds(HID, HID)]),
            (3, wd_hbm, wd.at[e, pl.ds(0, D)]),
        ):
            loads.append(pltpu.make_async_copy(src.at[e], dst, in_sem.at[n]))
    loads[0].start()
    loads[1].start()
    tok[pl.ds(D, PADDED - D), :] = jnp.zeros((PADDED - D, TOK), BF16)
    og[pl.ds(D, PADDED - D), :] = jnp.zeros((PADDED - D, TOK), BF16)

    lifted = jnp.exp(logits_ref[...])
    weights = lifted / jnp.sum(lifted, 0, keepdims=True)
    ids = ids_ref[...]
    row = iota((256, TOK), 0)
    spot = row & 15
    earlier = ones_where(iota((TOK, TOK), 0) < iota((TOK, TOK), 1))

    def select(expert, rank):
        named = jnp.zeros((256, TOK), F32)
        weigh = jnp.zeros((256, TOK), F32)
        for p in range(4):
            same = ids[p : p + 1, :] == expert
            named = jnp.where(same, 1.0, named)
            weigh = jnp.where(same, weights[p : p + 1, :], weigh)
        before = dg(named.astype(BF16), earlier, 1, 0)
        chosen = (before == rank.astype(F32)) & (named > 0.5)
        return chosen, jnp.where(chosen, weigh, 0.0)

    second = jnp.where(spot >= RANKS, 1, 0)
    base = 4 * (row >> 4) + 2 * par
    main_expert = base + second
    fold_expert = base + 1
    base_back = 4 * (row >> 4) + 2 * (1 - par)
    main_back = base_back + second
    fold_back = base_back + 1
    main, main_w = select(main_expert, spot - RANKS * second)
    fold, fold_w = select(fold_expert, 6 + (spot & 3))
    sel_main[...] = ones_where(main)
    for k in range(3):
        sel_fold[:, k * TOK : (k + 1) * TOK] = ones_where(fold & ((spot >> 2) == k))
    start = pl.multiple_of(c * WIDE, WIDE)

    def gather(a, source):
        loads[a].wait()
        whole = dg(sel_main[...], source[pl.ds(start, WIDE), :], 1, 1)
        folded = jnp.zeros((256, GROUP), F32)
        for k in range(3):
            feats = source[pl.ds(pl.multiple_of(start + k * GROUP, GROUP), GROUP), :]
            folded += dg(sel_fold[:, k * TOK : (k + 1) * TOK], feats, 1, 1)
        if a == 1:
            whole = jnp.sum(main_w, 1, keepdims=True) * whole
            some = jnp.where((spot >> 2) < 3, fold_w, 0.0)
            folded = jnp.sum(some, 1, keepdims=True) * folded
        send_slab[a, :, 0:WIDE] = whole.astype(BF16)
        send_slab[a, :, WIDE:MSG] = folded.astype(BF16)

    def dispatch(a, i):
        return pltpu.make_async_remote_copy(
            src_ref=send_slab.at[a, slab_rows(peer(i))],
            dst_ref=cat.at[a, 0, c, slab_rows(me)],
            send_sem=xy_s.at[a], recv_sem=xy_r.at[a, i],
            device_id=(d, peer(i)), device_id_type=MESH,
        )

    def arrive(a, i):
        return pltpu.make_async_remote_copy(
            src_ref=send_slab.at[a, slab_rows(peer(i))],
            dst_ref=cat.at[a, 0, c, slab_rows(origin(i))],
            send_sem=xy_s.at[a], recv_sem=xy_r.at[a, i],
            device_id=(d, peer(i)), device_id_type=MESH,
        )

    def along_z(a, s):
        side = s // 8
        return pltpu.make_async_remote_copy(
            src_ref=cat.at[a, 0, c, slab_rows(s)],
            dst_ref=cat.at[a, 1, c, slab_rows(s)],
            send_sem=zf_s.at[a], recv_sem=zf_r.at[a, side],
            device_id=(lax.rem(z + 1 - 2 * side + 8, 8) * 2 + c, me), device_id_type=MESH,
        )

    def along_z_all(a, side):
        eight = pl.ds(8 * SLAB * side, 8 * SLAB)
        return pltpu.make_async_remote_copy(
            src_ref=cat.at[a, 0, c, eight], dst_ref=cat.at[a, 1, c, eight],
            send_sem=zf_s.at[a], recv_sem=zf_r.at[a, side],
            device_id=down if side else up, device_id_type=MESH,
        )

    def to_sibling(a, o, s, count=1):
        some = pl.ds(pl.multiple_of(s * SLAB, SLAB), count * SLAB)
        return pltpu.make_async_remote_copy(
            src_ref=cat.at[a, o, c, some], dst_ref=cat.at[a, o, c, some],
            send_sem=cf_s.at[a, o], recv_sem=cf_r.at[a, o],
            device_id=sib, device_id_type=MESH,
        )

    def from_sibling(a, o):
        return pltpu.make_async_remote_copy(
            src_ref=cat.at[a, o, c], dst_ref=cat.at[a, o, 1 - c],
            send_sem=cf_s.at[a, o], recv_sem=cf_r.at[a, o],
            device_id=sib, device_id_type=MESH,
        )

    def loop(lo, hi, body):
        def step(i, carry):
            body(i)
            return carry

        lax.fori_loop(lo, hi, step, 0)

    def turn(j):
        return (jnp.where(j < 8, FIRST, LAST) >> (4 * lax.rem(j, 8))) & 15

    gather(0, tok)
    pl.semaphore_wait(barrier, 30)
    loop(0, 15, lambda j: dispatch(0, turn(j)).start())
    cat[0, 0, c, slab_rows(me), :] = send_slab[0, slab_rows(me), :]
    along_z(0, me).start()
    to_sibling(0, 0, me).start()
    for load in loads[2:]:
        load.start()
    gather(1, og)
    cat[1, 0, c, slab_rows(me), :] = send_slab[1, slab_rows(me), :]

    for e in range(4):
        wgu[e, pl.ds(D, WIDE - HALF), :] = jnp.zeros((WIDE - HALF, 2 * HID), BF16)
        wd[e, pl.ds(D, WIDE - HALF), :] = jnp.zeros((WIDE - HALF, HID), BF16)
    main, main_w = select(main_back, spot - RANKS * second)
    fold, fold_w = select(fold_back, 6 + (spot & 3))
    comb_hi[0] = main_w.astype(BF16)
    comb_lo[0] = (main_w - main_w.astype(BF16).astype(F32)).astype(BF16)
    comb_one[0] = ones_where(main)
    for k in range(3):
        here = (spot >> 2) == k
        w_here = jnp.where(here, fold_w, 0.0)
        comb_hi[1 + k] = w_here.astype(BF16)
        comb_lo[1 + k] = (w_here - w_here.astype(BF16).astype(F32)).astype(BF16)
        comb_one[1 + k] = ones_where(fold & here)

    n = iota((PAIR, 256), 0)
    i = iota((PAIR, 256), 1)
    later = jnp.where(n >= ROWS, 1, 0)
    m = n - ROWS * later
    s = (m * 6554) >> 16
    q = m - RANKS * s + RANKS * later
    grp[0] = ones_where((i == s * SLAB + q) & (q < 16))
    for k in range(3):
        grp[1 + k] = ones_where((i == s * SLAB + 4 * k + q - 16) & (q >= 16))
    n = iota((256, PAIR), 1)
    i = iota((256, PAIR), 0)
    later = jnp.where(n >= ROWS, 1, 0)
    m = n - ROWS * later
    s = (m * 6554) >> 16
    q = m - RANKS * s + RANKS * later
    ungrp[0] = ones_where((i == s * SLAB + q) & (q < 16))
    for k in range(3):
        ungrp[1 + k] = ones_where((i == s * SLAB + 4 * k + q - 16) & (q >= 16))
    line = iota((4 * BROWS, PART), 0)
    block = (line * 683) >> 16
    inner = line - BROWS * block
    place = BLK * block + inner
    for f in range(2):
        blksel[f] = ones_where((iota((4 * BROWS, PART), 1) == place + 8 * f) & (inner < BLK))

    def first_hop(a, lo, hi):
        def body(j):
            i = turn(j)
            arrive(a, i).wait_recv()

            along_z(a, origin(i)).start()
            to_sibling(a, 0, origin(i)).start()

        loop(lo, hi, body)

    def second_hop(a):
        for side in range(2):
            along_z_all(a, side).wait_recv()
            to_sibling(a, 1, 8 * side, 8).start()

    def regroup(a, o):
        from_sibling(a, o).wait_recv()
        for h in range(2):
            folded = cat[a, o, h, :, WIDE:MSG]
            for k in range(3):
                value = dg(grp[0], cat[a, o, h, :, k * GROUP : (k + 1) * GROUP], 1, 0)
                value += dg(grp[1 + k], folded, 1, 0)
                rows[a, o, :, h * WIDE + k * GROUP : h * WIDE + (k + 1) * GROUP] = value.astype(BF16)

    def expert_of(o, le):
        return 2 * (par + o - 2 * par * o) + le

    def of_expert(le):
        return pl.ds(pl.multiple_of(le * ROWS, ROWS), ROWS)

    def feats(far, f):
        side = 1 - c if far else c
        return pl.ds(pl.multiple_of(side * HALF + f * STEP, 16), PART)

    def to_core(a, f, o):
        return pltpu.make_async_remote_copy(
            src_ref=part.at[a, 1, f, o], dst_ref=crecv.at[a, f, o],
            send_sem=rc_s.at[a], recv_sem=rc_r.at[a, f, o],
            device_id=sib, device_id_type=MESH,
        )

    def forward(o):
        regroup(0, o)

        def body(le):
            e = expert_of(o, le)
            r = of_expert(le)
            xe = rows[0, o, r, 0:D]
            both = dg(xe, wgu[e, pl.ds(0, D), :], 1, 0)
            pg = both[:, 0:HID]
            pu = both[:, HID : 2 * HID] + 1.0
            sg = jax.nn.sigmoid(1.702 * pg)
            ac = pg * sg
            sig[o, r, :] = sg
            pre[o, r, :] = pg
            act[o, r, :] = ac
            upp[o, r, :] = pu
            hid[o, r, :] = (ac * pu).astype(BF16)

        loop(0, 2, body)

    def outputs(o, f):
        def body(le):
            e = expert_of(o, le)
            r = of_expert(le)
            for far in range(2):
                value = dg(hid[o, r, :], wd[e, feats(far, f), :], 1, 1)
                part[0, far, f, o, r, :] = value.astype(BF16)

        loop(0, 2, body)
        to_core(0, f, o).start()

    def backward(o):
        regroup(1, o)

        def body(le):
            e = expert_of(o, le)
            r = of_expert(le)
            ge = rows[1, o, r, 0:D]
            hg = dg(ge, wd[e, pl.ds(0, D), :], 1, 0)
            sg, pg, ac, pu = sig[o, r, :], pre[o, r, :], act[o, r, :], upp[o, r, :]
            slope = sg + 1.702 * pg * sg * (1.0 - sg)
            ggu[o, r, 0:HID] = (hg * pu * slope).astype(BF16)
            ggu[o, r, HID : 2 * HID] = (hg * ac).astype(BF16)
            dot = jnp.sum(hid[o, r, :].astype(F32) * hg, 1, keepdims=True)
            dotc[o, r, :] = jnp.broadcast_to(dot, (ROWS, HID))

        loop(0, 2, body)

    def inputs(o, f):
        def body(le):
            e = expert_of(o, le)
            r = of_expert(le)
            for far in range(2):
                value = dg(ggu[o, r, :], wgu[e, feats(far, f), :], 1, 1)
                if f == 1:
                    dot = dotc[o, r, 0:1] if far == 0 else 0.0
                    value = jnp.where(iota((ROWS, PART), 1) == DOT_LANE, dot, value)
                part[1, far, f, o, r, :] = value.astype(BF16)

        loop(0, 2, body)
        to_core(1, f, o).start()

    def across(a, f, le):
        return pltpu.make_async_remote_copy(
            src_ref=zsend.at[a, f, le], dst_ref=zrecv.at[a, f, le],
            send_sem=rz_s.at[a], recv_sem=rz_r.at[a, f],
            device_id=up if le == 0 else down, device_id_type=MESH,
        )

    def reduce_far(a, f):
        to_core(a, f, 0).wait_recv()
        for le in range(2):
            r = pl.ds(le * ROWS, ROWS)
            total = part[a, 0, f, 0, r, :].astype(F32) + crecv[a, f, 0, r, :].astype(F32)
            zsend[a, f, le] = total.astype(BF16)
            across(a, f, le).start()

    def give_back(a, f, i):
        return pltpu.make_async_remote_copy(
            src_ref=slab.at[a, f, slab_rows(peer(i))],
            dst_ref=back.at[a, f, slab_rows(me)],
            send_sem=bk_s.at[a, f], recv_sem=bk_r.at[a, f],
            device_id=(d, peer(i)), device_id_type=MESH,
        )

    def all_back(a, f):
        fifteen = pl.ds(0, 15 * SLAB)
        return pltpu.make_async_remote_copy(
            src_ref=slab.at[a, f, fifteen], dst_ref=back.at[a, f, fifteen],
            send_sem=bk_s.at[a, f], recv_sem=bk_r.at[a, f],
            device_id=sib, device_id_type=MESH,
        )

    def reduce_near(a, f):
        to_core(a, f, 1).wait_recv()
        totals = []
        pltpu.make_async_remote_copy(
            src_ref=zsend.at[a, f], dst_ref=zrecv.at[a, f],
            send_sem=rz_s.at[a], recv_sem=rz_r.at[a, f],
            device_id=up, device_id_type=MESH,
        ).wait_recv()
        for le in range(2):
            r = pl.ds(le * ROWS, ROWS)
            total = part[a, 0, f, 1, r, :].astype(F32) + crecv[a, f, 1, r, :].astype(F32)
            totals.append((total + zrecv[a, f, le].astype(F32)).astype(BF16))
        both = jnp.concatenate(totals, 0)
        slab[a, f, :, 0:PART] = dg(ungrp[0], both, 1, 0).astype(BF16)
        folded = jnp.zeros((256, TOK), F32)
        for k in range(3):
            folded += dg(ungrp[1 + k], both[:, k * TOK : (k + 1) * TOK], 1, 0)
        slab[a, f, :, PART:BACK] = folded.astype(BF16)
        back[a, f, slab_rows(me), :] = slab[a, f, slab_rows(me), :]
        loop(1, 16, lambda i: give_back(a, f, i).start())

    def block_owner(k):
        return (4 * c + k // 2) * 2 + k % 2

    def hand_out(a, k):
        return pltpu.make_async_remote_copy(
            src_ref=blocks.at[a, k], dst_ref=frecv.at[a, z],
            send_sem=fb_s.at[a], recv_sem=fb_r.at[a],
            device_id=(block_owner(k), me), device_id_type=MESH,
        )

    def handed(a, count):
        return pltpu.make_async_remote_copy(
            src_ref=blocks.at[a, pl.ds(0, count)], dst_ref=frecv.at[a, pl.ds(0, count)],
            send_sem=fb_s.at[a], recv_sem=fb_r.at[a],
            device_id=sib, device_id_type=MESH,
        )

    def tell(i):
        return pltpu.make_async_remote_copy(
            src_ref=dots.at[d], dst_ref=dots.at[d],
            send_sem=dt_s, recv_sem=dt_r,
            device_id=(lax.rem(d + i, 16), me), device_id_type=MESH,
        )

    def told():
        return pltpu.make_async_remote_copy(
            src_ref=dots.at[pl.ds(0, 15)], dst_ref=dots.at[pl.ds(0, 15)],
            send_sem=dt_s, recv_sem=dt_r,
            device_id=sib, device_id_type=MESH,
        )

    def combine(a, f):
        all_back(a, f).wait_recv()
        if a == 1 and f == 1:
            main_dot = back[1, 1, :, DOT_LANE : DOT_LANE + 1].astype(F32)
            lane = DOT_LANE + TOK
            fold_dot = back[1, 1, :, lane : lane + 1].astype(F32)
            main_dot = jnp.where(comb_one[0].astype(F32) > 0.5, main_dot, 0.0)
            fold_dot = jnp.where(comb_one[3].astype(F32) > 0.5, fold_dot, 0.0)
            lines = []
            for p in range(4):
                mine_p = jnp.where(ids[p : p + 1, :] == main_back, main_dot, 0.0)
                mine_p += jnp.where(ids[p : p + 1, :] == fold_back, fold_dot, 0.0)
                lines.append(jnp.sum(mine_p, 0, keepdims=True))
            dots[d] = jnp.concatenate(lines + [jnp.zeros((4, TOK), F32)], 0)
            loop(1, 16, lambda i: tell(i).start())
        tables = (comb_hi, comb_lo) if a == 0 else (comb_one,)
        value = jnp.zeros((TOK, PART), F32)
        for table in tables:
            value += dg(table[0], back[a, f, :, 0:PART], 0, 0)
            value += jnp.concatenate(
                [dg(table[1 + k], back[a, f, :, PART:BACK], 0, 0) for k in range(3)], 1
            )
        total = dg(blksel[f], value.astype(BF16), 1, 1).astype(BF16)
        for k in range(4):
            blocks[a, 4 * f + k] = total[k * BROWS : (k + 1) * BROWS, :]

        def body(k):
            @pl.when(block_owner(k) != d)
            def _():
                hand_out(a, k).start()

            @pl.when(block_owner(k) == d)
            def _():
                frecv[a, z] = blocks[a, k]

        loop(4 * f, 4 * f + 4, body)

    inside = lax.div(z, 4) == c

    def finish(a, out_ref):
        @pl.when(inside)
        def _():
            handed(a, 7).wait_recv()

        @pl.when(jnp.logical_not(inside))
        def _():
            handed(a, 8).wait_recv()

        total = frecv[a, 0].astype(F32)
        for zz in range(1, 8):
            total += frecv[a, zz].astype(F32)
        out_ref[...] = total[0:BLK, :].astype(BF16)

    def store(o, le, n):
        out = (gg_hbm, gu_hbm, gd_hbm)[n]
        e = expert_of(o, le)
        return pltpu.make_async_copy(grads.at[n, e], out.at[e], out_sem.at[n])

    def weight_grads(o):
        def body(le):
            e = expert_of(o, le)
            r = of_expert(le)
            both = dg(rows[0, o, r, 0:D], ggu[o, r, :], 0, 0)
            grads[0, e] = both[:, 0:HID].astype(BF16)
            grads[1, e] = both[:, HID : 2 * HID].astype(BF16)
            grads[2, e] = dg(rows[1, o, r, 0:D], hid[o, r, :], 0, 0).astype(BF16)
            for n in range(3):
                store(o, le, n).start()

        loop(0, 2, body)

    first_hop(0, 0, 15)
    loop(0, 15, lambda j: dispatch(1, turn(j)).start())
    along_z(1, me).start()
    to_sibling(1, 0, me).start()
    for n, w in ((2, wgu), (3, wd)):
        all_rows = w.at[:, pl.ds(0, D)]
        pltpu.make_async_copy(all_rows, all_rows, in_sem.at[n]).wait()
    forward(0)
    outputs(0, 0)
    outputs(0, 1)
    second_hop(0)
    first_hop(1, 0, 5)
    reduce_far(0, 0)
    reduce_far(0, 1)
    forward(1)
    first_hop(1, 5, 10)
    outputs(1, 0)
    outputs(1, 1)
    first_hop(1, 10, 15)
    backward(0)
    inputs(0, 0)
    inputs(0, 1)
    reduce_near(0, 0)
    reduce_near(0, 1)
    reduce_far(1, 0)
    reduce_far(1, 1)
    weight_grads(0)
    second_hop(1)
    backward(1)
    inputs(1, 0)
    inputs(1, 1)
    reduce_near(1, 0)
    reduce_near(1, 1)
    combine(0, 0)
    combine(0, 1)
    weight_grads(1)
    combine(1, 0)
    combine(1, 1)
    finish(0, mixed_ref)
    finish(1, igrad_ref)
    told().wait_recv()
    total = dots[0]
    for k in range(1, 16):
        total += dots[k]
    dot = total[0:4, :]
    rgrad_ref[...] = dot - weights * jnp.sum(dot, 0, keepdims=True)

    told().wait_send()
    for a in range(2):
        fifteen = pl.ds(0, 15 * SLAB)
        pltpu.make_async_remote_copy(
            src_ref=send_slab.at[a, fifteen], dst_ref=cat.at[a, 0, c, fifteen],
            send_sem=xy_s.at[a], recv_sem=xy_r.at[a, 0],
            device_id=sib, device_id_type=MESH,
        ).wait_send()
        pltpu.make_async_remote_copy(
            src_ref=cat.at[a, 0, c], dst_ref=cat.at[a, 1, c],
            send_sem=zf_s.at[a], recv_sem=zf_r.at[a, 0],
            device_id=sib, device_id_type=MESH,
        ).wait_send()
        pltpu.make_async_remote_copy(
            src_ref=part.at[a, 1], dst_ref=crecv.at[a],
            send_sem=rc_s.at[a], recv_sem=rc_r.at[a, 0, 0],
            device_id=sib, device_id_type=MESH,
        ).wait_send()
        pltpu.make_async_remote_copy(
            src_ref=zsend.at[a], dst_ref=zrecv.at[a],
            send_sem=rz_s.at[a], recv_sem=rz_r.at[a, 0],
            device_id=sib, device_id_type=MESH,
        ).wait_send()
        for f in range(2):
            from_sibling(a, f).wait_send()
            all_back(a, f).wait_send()

        @pl.when(inside)
        def _():
            handed(a, 7).wait_send()

        @pl.when(jnp.logical_not(inside))
        def _():
            handed(a, 8).wait_send()

    for n, out in enumerate((gg_hbm, gu_hbm, gd_hbm)):
        pltpu.make_async_copy(grads.at[n], out, out_sem.at[n]).wait()


def deliver(
    mixed_in, igrad_in, rgrad_in, gg_in, gu_in, gd_in,
    mixed_out, igrad_out, rgrad_out, gg_out, gu_out, gd_out, sem,
):
    pairs = ((gg_in, gg_out), (gu_in, gu_out), (gd_in, gd_out))
    writes = []
    for n, (src, dst) in enumerate(pairs):
        for e in range(4):
            writes.append(pltpu.make_async_copy(src.at[e], dst.at[e], sem.at[n, e]))
    for write in writes:
        write.start()
    mixed_out[...] = mixed_in[...]
    igrad_out[...] = igrad_in[...]
    rgrad_out[...] = rgrad_in[...]
    for write in writes:
        write.wait()


def on_device(tokens, output_grad, router_logits, expert_ids, w_gate, w_up, w_down):
    anywhere = pl.BlockSpec(memory_space=pl.ANY)
    vmem = pl.BlockSpec(memory_space=pltpu.VMEM)
    dma = pltpu.SemaphoreType.DMA
    weight = jax.ShapeDtypeStruct((4, D, HID), BF16)
    kept = pltpu.VMEM((4, D, HID), BF16)
    part_kept = pltpu.VMEM((BLK, TOK), BF16)
    block = jax.ShapeDtypeStruct((BLK, TOK), BF16)
    mixed, igrad, rgrad, gg, gu, gd = pl.pallas_call(
        kernel,
        out_shape=(part_kept, part_kept, pltpu.VMEM((4, TOK), F32), kept, kept, kept),
        in_specs=[anywhere, anywhere, vmem, vmem, anywhere, anywhere, anywhere],
        out_specs=(vmem, vmem, vmem, anywhere, anywhere, anywhere),
        scratch_shapes=[
            pltpu.VMEM((PADDED, TOK), BF16),
            pltpu.VMEM((PADDED, TOK), BF16),
            pltpu.VMEM((4, D + WIDE - HALF, 2 * HID), BF16),
            pltpu.VMEM((4, D + WIDE - HALF, HID), BF16),
            pltpu.VMEM((2, 256, MSG), BF16),
            pltpu.VMEM((2, 2, 2, 256, MSG), BF16),
            pltpu.VMEM((2, 2, PAIR, PADDED), BF16),
            pltpu.VMEM((256, TOK), BF16),
            pltpu.VMEM((256, 3 * TOK), BF16),
            pltpu.VMEM((4, 256, TOK), BF16),
            pltpu.VMEM((4, 256, TOK), BF16),
            pltpu.VMEM((4, 256, TOK), BF16),
            pltpu.VMEM((4, PAIR, 256), BF16),
            pltpu.VMEM((4, 256, PAIR), BF16),
            pltpu.VMEM((2, 4 * BROWS, PART), BF16),
            pltpu.VMEM((2, PAIR, HID), F32),
            pltpu.VMEM((2, PAIR, HID), F32),
            pltpu.VMEM((2, PAIR, HID), F32),
            pltpu.VMEM((2, PAIR, HID), F32),
            pltpu.VMEM((2, PAIR, HID), BF16),
            pltpu.VMEM((2, PAIR, 2 * HID), BF16),
            pltpu.VMEM((2, PAIR, HID), F32),
            pltpu.VMEM((2, 2, 2, 2, PAIR, PART), BF16),
            pltpu.VMEM((2, 2, 2, PAIR, PART), BF16),
            pltpu.VMEM((2, 2, 2, ROWS, PART), BF16),
            pltpu.VMEM((2, 2, 2, ROWS, PART), BF16),
            pltpu.VMEM((2, 2, 256, BACK), BF16),
            pltpu.VMEM((2, 2, 256, BACK), BF16),
            pltpu.VMEM((2, 8, BROWS, TOK), BF16),
            pltpu.VMEM((2, 8, BROWS, TOK), BF16),
            pltpu.VMEM((16, 8, TOK), F32),
            pltpu.VMEM((3, 4, D, HID), BF16),
            dma((4,)),
            dma((2,)), dma((2, 16)),
            dma((2,)), dma((2, 2)),
            dma((2, 2)), dma((2, 2)),
            dma((2,)), dma((2, 2, 2)),
            dma((2,)), dma((2, 2)),
            dma((2, 2)), dma((2, 2)),
            dma((2,)), dma((2,)),
            dma(()), dma(()),
            dma((3,)),
        ],
        compiler_params=pltpu.CompilerParams(
            collective_id=0, has_side_effects=True, vmem_limit_bytes=59 * 2**20
        ),
        cost_estimate=pl.CostEstimate(
            flops=2 * 9 * 640 * D * HID, bytes_accessed=9 * 10**6, transcendentals=640 * HID
        ),
        name="moe_layer",
    )(
        tokens.T, output_grad.T, router_logits.T, expert_ids.T,
        w_gate, w_up, jnp.swapaxes(w_down, 1, 2),
    )
    mixed, igrad, rgrad, gg, gu, gd = pl.pallas_call(
        deliver,
        out_shape=(block, block, jax.ShapeDtypeStruct((4, TOK), F32), weight, weight, weight),
        in_specs=[vmem, vmem, vmem, vmem, vmem, vmem],
        out_specs=(vmem, vmem, vmem, anywhere, anywhere, anywhere),
        scratch_shapes=[dma((3, 4))],
        compiler_params=pltpu.CompilerParams(vmem_limit_bytes=16 * 2**20),
        cost_estimate=pl.CostEstimate(flops=0, bytes_accessed=9 * 10**6, transcendentals=0),
        name="deliver",
    )(mixed, igrad, rgrad, gg, gu, gd)
    return mixed.T, igrad.T, rgrad.T, gg, gu, jnp.swapaxes(gd, 1, 2)


def solution(mesh):
    in_specs = (
        P("expert", None),
        P("expert", None),
        P("expert", None),
        P("expert", None),
        P("expert", None, "dp"),
        P("expert", None, "dp"),
        P("expert", "dp", None),
    )
    out_specs = (
        P("expert", "dp"),
        P("expert", "dp"),
        P("expert", None),
        P("expert", None, "dp"),
        P("expert", None, "dp"),
        P("expert", "dp", None),
    )
    return jax.shard_map(
        on_device, mesh=mesh, in_specs=in_specs, out_specs=out_specs, check_vma=False
    )
```

```python
import jax
import jax.numpy as jnp
import numpy as np
from jax import lax
from jax.experimental import pallas as pl
from jax.experimental.pallas import tpu as pltpu
from jax.sharding import PartitionSpec as P

MESH = pl.DeviceIdType.MESH
F32 = jnp.float32
BF16 = jnp.bfloat16

D = 1440
HALF = 720
WIDE = 768
PADDED = 1536
HID = 128
TOK = 128
RANKS = 10
SRC = 16
ROWS = SRC * RANKS
PAIR = 2 * ROWS
SLAB = 16
MSG = 1024
GROUP = 256
PART = 384
STEP = 352
BACK = 512
DOT_LANE = 376
ORDER = (1, 12, 3, 4, 2, 8, 5, 15, 7, 13, 6, 14, 9, 11, 10)
FIRST = int(np.int32(np.uint32(sum(i << (4 * j) for j, i in enumerate(ORDER[:8])))))
LAST = sum(i << (4 * j) for j, i in enumerate(ORDER[8:]))
BLK = 90
BROWS = 96


def dg(a, b, ca, cb):
    return lax.dot_general(a, b, (((ca,), (cb,)), ((), ())), preferred_element_type=F32)


def iota(shape, dim):
    return lax.broadcasted_iota(jnp.int32, shape, dim)


def ones_where(mask):
    return jnp.where(mask, 1.0, 0.0).astype(BF16)


def kernel(
    tok_hbm, og_hbm, logits_ref, ids_ref, wg_hbm, wu_hbm, wd_hbm,
    mixed_ref, igrad_ref, rgrad_ref, gg_hbm, gu_hbm, gd_hbm,
    tok, og, wgu, wd,
    send_slab, cat, rows, sel_main, sel_fold, comb_hi, comb_lo, comb_one,
    grp, ungrp, blksel,
    sig, pre, act, upp, hid, ggu, dotc,
    part, crecv, zsend, zrecv, slab, back, blocks, frecv, dots,
    grads,
    in_sem, xy_s, xy_r, zf_s, zf_r, cf_s, cf_r, rc_s, rc_r, rz_s, rz_r,
    bk_s, bk_r, fb_s, fb_r, dt_s, dt_r, out_sem,
):
    d = lax.axis_index("dp")
    me = lax.axis_index("expert")
    z, c = lax.div(d, 2), lax.rem(d, 2)
    x, y = lax.div(me, 4), lax.rem(me, 4)
    par = lax.rem(z, 2)
    sib = (z * 2 + 1 - c, me)
    up = (lax.rem(z + 1, 8) * 2 + c, me)
    down = (lax.rem(z + 7, 8) * 2 + c, me)

    def peer(i):
        return lax.rem(x + i // 4, 4) * 4 + lax.rem(y + i % 4, 4)

    def origin(i):
        return lax.rem(x + 4 - i // 4, 4) * 4 + lax.rem(y + 4 - i % 4, 4)

    def slab_rows(s):
        return pl.ds(pl.multiple_of(s * SLAB, SLAB), SLAB)

    barrier = pltpu.get_barrier_semaphore()

    def greet(i, carry):
        pl.semaphore_signal(barrier, inc=1, device_id=(d, peer(i)), device_id_type=MESH)
        pl.semaphore_signal(
            barrier, inc=1, device_id=(lax.rem(d + i, 16), me), device_id_type=MESH
        )
        return carry

    lax.fori_loop(1, 16, greet, 0)

    loads = [
        pltpu.make_async_copy(tok_hbm, tok.at[pl.ds(0, D)], in_sem.at[0]),
        pltpu.make_async_copy(og_hbm, og.at[pl.ds(0, D)], in_sem.at[1]),
    ]
    for e in range(4):
        for n, src, dst in (
            (2, wg_hbm, wgu.at[e, pl.ds(0, D), pl.ds(0, HID)]),
            (2, wu_hbm, wgu.at[e, pl.ds(0, D), pl.ds(HID, HID)]),
            (3, wd_hbm, wd.at[e, pl.ds(0, D)]),
        ):
            loads.append(pltpu.make_async_copy(src.at[e], dst, in_sem.at[n]))
    loads[0].start()
    loads[1].start()
    tok[pl.ds(D, PADDED - D), :] = jnp.zeros((PADDED - D, TOK), BF16)
    og[pl.ds(D, PADDED - D), :] = jnp.zeros((PADDED - D, TOK), BF16)

    lifted = jnp.exp(logits_ref[...])
    weights = lifted / jnp.sum(lifted, 0, keepdims=True)
    ids = ids_ref[...]
    row = iota((256, TOK), 0)
    spot = row & 15
    earlier = ones_where(iota((TOK, TOK), 0) < iota((TOK, TOK), 1))

    def select(expert, rank):
        named = jnp.zeros((256, TOK), F32)
        weigh = jnp.zeros((256, TOK), F32)
        for p in range(4):
            same = ids[p : p + 1, :] == expert
            named = jnp.where(same, 1.0, named)
            weigh = jnp.where(same, weights[p : p + 1, :], weigh)
        before = dg(named.astype(BF16), earlier, 1, 0)
        chosen = (before == rank.astype(F32)) & (named > 0.5)
        return chosen, jnp.where(chosen, weigh, 0.0)

    second = jnp.where(spot >= RANKS, 1, 0)
    base = 4 * (row >> 4) + 2 * par
    main_expert = base + second
    fold_expert = base + 1
    base_back = 4 * (row >> 4) + 2 * (1 - par)
    main_back = base_back + second
    fold_back = base_back + 1
    main, main_w = select(main_expert, spot - RANKS * second)
    fold, fold_w = select(fold_expert, 6 + (spot & 3))
    sel_main[...] = ones_where(main)
    for k in range(3):
        sel_fold[:, k * TOK : (k + 1) * TOK] = ones_where(fold & ((spot >> 2) == k))
    start = pl.multiple_of(c * WIDE, WIDE)

    def gather(a, source):
        loads[a].wait()
        whole = dg(sel_main[...], source[pl.ds(start, WIDE), :], 1, 1)
        folded = jnp.zeros((256, GROUP), F32)
        for k in range(3):
            feats = source[pl.ds(pl.multiple_of(start + k * GROUP, GROUP), GROUP), :]
            folded += dg(sel_fold[:, k * TOK : (k + 1) * TOK], feats, 1, 1)
        if a == 1:
            whole = jnp.sum(main_w, 1, keepdims=True) * whole
            some = jnp.where((spot >> 2) < 3, fold_w, 0.0)
            folded = jnp.sum(some, 1, keepdims=True) * folded
        send_slab[a, :, 0:WIDE] = whole.astype(BF16)
        send_slab[a, :, WIDE:MSG] = folded.astype(BF16)

    def dispatch(a, i):
        return pltpu.make_async_remote_copy(
            src_ref=send_slab.at[a, slab_rows(peer(i))],
            dst_ref=cat.at[a, 0, c, slab_rows(me)],
            send_sem=xy_s.at[a], recv_sem=xy_r.at[a, i],
            device_id=(d, peer(i)), device_id_type=MESH,
        )

    def arrive(a, i):
        return pltpu.make_async_remote_copy(
            src_ref=send_slab.at[a, slab_rows(peer(i))],
            dst_ref=cat.at[a, 0, c, slab_rows(origin(i))],
            send_sem=xy_s.at[a], recv_sem=xy_r.at[a, i],
            device_id=(d, peer(i)), device_id_type=MESH,
        )

    def along_z(a, s):
        side = s // 8
        return pltpu.make_async_remote_copy(
            src_ref=cat.at[a, 0, c, slab_rows(s)],
            dst_ref=cat.at[a, 1, c, slab_rows(s)],
            send_sem=zf_s.at[a], recv_sem=zf_r.at[a, side],
            device_id=(lax.rem(z + 1 - 2 * side + 8, 8) * 2 + c, me), device_id_type=MESH,
        )

    def along_z_all(a, side):
        eight = pl.ds(8 * SLAB * side, 8 * SLAB)
        return pltpu.make_async_remote_copy(
            src_ref=cat.at[a, 0, c, eight], dst_ref=cat.at[a, 1, c, eight],
            send_sem=zf_s.at[a], recv_sem=zf_r.at[a, side],
            device_id=down if side else up, device_id_type=MESH,
        )

    def to_sibling(a, o, s, count=1):
        some = pl.ds(pl.multiple_of(s * SLAB, SLAB), count * SLAB)
        return pltpu.make_async_remote_copy(
            src_ref=cat.at[a, o, c, some], dst_ref=cat.at[a, o, c, some],
            send_sem=cf_s.at[a, o], recv_sem=cf_r.at[a, o],
            device_id=sib, device_id_type=MESH,
        )

    def from_sibling(a, o):
        return pltpu.make_async_remote_copy(
            src_ref=cat.at[a, o, c], dst_ref=cat.at[a, o, 1 - c],
            send_sem=cf_s.at[a, o], recv_sem=cf_r.at[a, o],
            device_id=sib, device_id_type=MESH,
        )

    def loop(lo, hi, body):
        def step(i, carry):
            body(i)
            return carry

        lax.fori_loop(lo, hi, step, 0)

    def turn(j):
        return (jnp.where(j < 8, FIRST, LAST) >> (4 * lax.rem(j, 8))) & 15

    gather(0, tok)
    pl.semaphore_wait(barrier, 30)
    loop(0, 15, lambda j: dispatch(0, turn(j)).start())
    cat[0, 0, c, slab_rows(me), :] = send_slab[0, slab_rows(me), :]
    along_z(0, me).start()
    to_sibling(0, 0, me).start()
    for load in loads[2:]:
        load.start()
    gather(1, og)
    cat[1, 0, c, slab_rows(me), :] = send_slab[1, slab_rows(me), :]

    for e in range(4):
        wgu[e, pl.ds(D, WIDE - HALF), :] = jnp.zeros((WIDE - HALF, 2 * HID), BF16)
        wd[e, pl.ds(D, WIDE - HALF), :] = jnp.zeros((WIDE - HALF, HID), BF16)
    for o in range(2):
        if o == 1:
            main, main_w = select(main_back, spot - RANKS * second)
            fold, fold_w = select(fold_back, 6 + (spot & 3))
        comb_hi[o, 0] = main_w.astype(BF16)
        comb_lo[o, 0] = (main_w - main_w.astype(BF16).astype(F32)).astype(BF16)
        for k in range(3):
            w_here = jnp.where((spot >> 2) == k, fold_w, 0.0)
            comb_hi[o, 1 + k] = w_here.astype(BF16)
            comb_lo[o, 1 + k] = (w_here - w_here.astype(BF16).astype(F32)).astype(BF16)
    comb_one[0] = ones_where(main)
    for k in range(3):
        comb_one[1 + k] = ones_where(fold & ((spot >> 2) == k))

    n = iota((PAIR, 256), 0)
    i = iota((PAIR, 256), 1)
    later = jnp.where(n >= ROWS, 1, 0)
    m = n - ROWS * later
    s = (m * 6554) >> 16
    q = m - RANKS * s + RANKS * later
    grp[0] = ones_where((i == s * SLAB + q) & (q < 16))
    for k in range(3):
        grp[1 + k] = ones_where((i == s * SLAB + 4 * k + q - 16) & (q >= 16))
    n = iota((256, PAIR), 1)
    i = iota((256, PAIR), 0)
    later = jnp.where(n >= ROWS, 1, 0)
    m = n - ROWS * later
    s = (m * 6554) >> 16
    q = m - RANKS * s + RANKS * later
    ungrp[0] = ones_where((i == s * SLAB + q) & (q < 16))
    for k in range(3):
        ungrp[1 + k] = ones_where((i == s * SLAB + 4 * k + q - 16) & (q >= 16))
    line = iota((4 * BROWS, PART), 0)
    block = (line * 683) >> 16
    inner = line - BROWS * block
    place = BLK * block + inner
    for f in range(2):
        blksel[f] = ones_where((iota((4 * BROWS, PART), 1) == place + 8 * f) & (inner < BLK))

    def first_hop(a, lo, hi):
        def body(j):
            i = turn(j)
            arrive(a, i).wait_recv()

            along_z(a, origin(i)).start()
            to_sibling(a, 0, origin(i)).start()

        loop(lo, hi, body)

    def second_hop(a):
        for side in range(2):
            along_z_all(a, side).wait_recv()
            to_sibling(a, 1, 8 * side, 8).start()

    def regroup(a, o):
        from_sibling(a, o).wait_recv()
        for h in range(2):
            folded = cat[a, o, h, :, WIDE:MSG]
            for k in range(3):
                value = dg(grp[0], cat[a, o, h, :, k * GROUP : (k + 1) * GROUP], 1, 0)
                value += dg(grp[1 + k], folded, 1, 0)
                rows[a, o, :, h * WIDE + k * GROUP : h * WIDE + (k + 1) * GROUP] = value.astype(BF16)

    def expert_of(o, le):
        return 2 * (par + o - 2 * par * o) + le

    def of_expert(le):
        return pl.ds(pl.multiple_of(le * ROWS, ROWS), ROWS)

    def feats(far, f):
        side = 1 - c if far else c
        return pl.ds(pl.multiple_of(side * HALF + f * STEP, 16), PART)

    def to_core(a, f, o):
        return pltpu.make_async_remote_copy(
            src_ref=part.at[a, 1, f, o], dst_ref=crecv.at[a, f, o],
            send_sem=rc_s.at[a], recv_sem=rc_r.at[a, f, o],
            device_id=sib, device_id_type=MESH,
        )

    def forward(o):
        regroup(0, o)

        def body(le):
            e = expert_of(o, le)
            r = of_expert(le)
            xe = rows[0, o, r, 0:D]
            both = dg(xe, wgu[e, pl.ds(0, D), :], 1, 0)
            pg = both[:, 0:HID]
            pu = both[:, HID : 2 * HID] + 1.0
            sg = jax.nn.sigmoid(1.702 * pg)
            ac = pg * sg
            sig[o, r, :] = sg
            pre[o, r, :] = pg
            act[o, r, :] = ac
            upp[o, r, :] = pu
            hid[o, r, :] = (ac * pu).astype(BF16)

        loop(0, 2, body)

    def outputs(o, f):
        def body(le):
            e = expert_of(o, le)
            r = of_expert(le)
            for far in range(2):
                value = dg(hid[o, r, :], wd[e, feats(far, f), :], 1, 1)
                part[0, far, f, o, r, :] = value.astype(BF16)

        loop(0, 2, body)
        to_core(0, f, o).start()

    def backward(o):
        regroup(1, o)

        def body(le):
            e = expert_of(o, le)
            r = of_expert(le)
            ge = rows[1, o, r, 0:D]
            hg = dg(ge, wd[e, pl.ds(0, D), :], 1, 0)
            sg, pg, ac, pu = sig[o, r, :], pre[o, r, :], act[o, r, :], upp[o, r, :]
            slope = sg + 1.702 * pg * sg * (1.0 - sg)
            ggu[o, r, 0:HID] = (hg * pu * slope).astype(BF16)
            ggu[o, r, HID : 2 * HID] = (hg * ac).astype(BF16)
            dot = jnp.sum(hid[o, r, :].astype(F32) * hg, 1, keepdims=True)
            dotc[o, r, :] = jnp.broadcast_to(dot, (ROWS, HID))

        loop(0, 2, body)

    def inputs(o, f):
        def body(le):
            e = expert_of(o, le)
            r = of_expert(le)
            for far in range(2):
                value = dg(ggu[o, r, :], wgu[e, feats(far, f), :], 1, 1)
                if f == 1:
                    dot = dotc[o, r, 0:1] if far == 0 else 0.0
                    value = jnp.where(iota((ROWS, PART), 1) == DOT_LANE, dot, value)
                part[1, far, f, o, r, :] = value.astype(BF16)

        loop(0, 2, body)
        to_core(1, f, o).start()

    def across(f, le):
        return pltpu.make_async_remote_copy(
            src_ref=zsend.at[f, le], dst_ref=zrecv.at[f, le],
            send_sem=rz_s, recv_sem=rz_r.at[f],
            device_id=up if le == 0 else down, device_id_type=MESH,
        )

    def reduce_far(f):
        to_core(1, f, 0).wait_recv()
        for le in range(2):
            r = pl.ds(le * ROWS, ROWS)
            total = part[1, 0, f, 0, r, :].astype(F32) + crecv[1, f, 0, r, :].astype(F32)
            zsend[f, le] = total.astype(BF16)
            across(f, le).start()

    def give_back(ch, f, i):
        return pltpu.make_async_remote_copy(
            src_ref=slab.at[ch, f, slab_rows(peer(i))],
            dst_ref=back.at[ch, f, slab_rows(me)],
            send_sem=bk_s.at[ch, f], recv_sem=bk_r.at[ch, f],
            device_id=(d, peer(i)), device_id_type=MESH,
        )

    def all_back(ch, f):
        fifteen = pl.ds(0, 15 * SLAB)
        return pltpu.make_async_remote_copy(
            src_ref=slab.at[ch, f, fifteen], dst_ref=back.at[ch, f, fifteen],
            send_sem=bk_s.at[ch, f], recv_sem=bk_r.at[ch, f],
            device_id=sib, device_id_type=MESH,
        )

    def across_all(f):
        return pltpu.make_async_remote_copy(
            src_ref=zsend.at[f], dst_ref=zrecv.at[f],
            send_sem=rz_s, recv_sem=rz_r.at[f],
            device_id=up, device_id_type=MESH,
        )

    def reduce_near(ch, f):
        a, o = ((0, 0), (0, 1), (1, 1))[ch]
        to_core(a, f, o).wait_recv()
        if ch == 2:
            across_all(f).wait_recv()
        totals = []
        for le in range(2):
            r = pl.ds(le * ROWS, ROWS)
            total = part[a, 0, f, o, r, :].astype(F32) + crecv[a, f, o, r, :].astype(F32)
            if ch == 2:
                total += zrecv[f, le].astype(F32)
            totals.append(total.astype(BF16))
        both = jnp.concatenate(totals, 0)
        slab[ch, f, :, 0:PART] = dg(ungrp[0], both, 1, 0).astype(BF16)
        folded = jnp.zeros((256, TOK), F32)
        for k in range(3):
            folded += dg(ungrp[1 + k], both[:, k * TOK : (k + 1) * TOK], 1, 0)
        slab[ch, f, :, PART:BACK] = folded.astype(BF16)
        back[ch, f, slab_rows(me), :] = slab[ch, f, slab_rows(me), :]
        loop(1, 16, lambda i: give_back(ch, f, i).start())

    def block_owner(k):
        return (4 * c + k // 2) * 2 + k % 2

    def hand_out(a, k):
        return pltpu.make_async_remote_copy(
            src_ref=blocks.at[a, k], dst_ref=frecv.at[a, z],
            send_sem=fb_s.at[a], recv_sem=fb_r.at[a],
            device_id=(block_owner(k), me), device_id_type=MESH,
        )

    def handed(a, count):
        return pltpu.make_async_remote_copy(
            src_ref=blocks.at[a, pl.ds(0, count)], dst_ref=frecv.at[a, pl.ds(0, count)],
            send_sem=fb_s.at[a], recv_sem=fb_r.at[a],
            device_id=sib, device_id_type=MESH,
        )

    def tell(i):
        return pltpu.make_async_remote_copy(
            src_ref=dots.at[d], dst_ref=dots.at[d],
            send_sem=dt_s, recv_sem=dt_r,
            device_id=(lax.rem(d + i, 16), me), device_id_type=MESH,
        )

    def told():
        return pltpu.make_async_remote_copy(
            src_ref=dots.at[pl.ds(0, 15)], dst_ref=dots.at[pl.ds(0, 15)],
            send_sem=dt_s, recv_sem=dt_r,
            device_id=sib, device_id_type=MESH,
        )

    def combine(a, f):
        for ch in (0, 1) if a == 0 else (2,):
            all_back(ch, f).wait_recv()
        if a == 1 and f == 1:
            main_dot = back[2, 1, :, DOT_LANE : DOT_LANE + 1].astype(F32)
            lane = DOT_LANE + TOK
            fold_dot = back[2, 1, :, lane : lane + 1].astype(F32)
            main_dot = jnp.where(comb_one[0].astype(F32) > 0.5, main_dot, 0.0)
            fold_dot = jnp.where(comb_one[3].astype(F32) > 0.5, fold_dot, 0.0)
            lines = []
            for p in range(4):
                mine_p = jnp.where(ids[p : p + 1, :] == main_back, main_dot, 0.0)
                mine_p += jnp.where(ids[p : p + 1, :] == fold_back, fold_dot, 0.0)
                lines.append(jnp.sum(mine_p, 0, keepdims=True))
            dots[d] = jnp.concatenate(lines + [jnp.zeros((4, TOK), F32)], 0)
            loop(1, 16, lambda i: tell(i).start())
        if a == 0:
            tables = [(t.at[o], o) for o in range(2) for t in (comb_hi, comb_lo)]
        else:
            tables = [(comb_one, 2)]
        value = jnp.zeros((TOK, PART), F32)
        for table, ch in tables:
            value += dg(table[0], back[ch, f, :, 0:PART], 0, 0)
            value += jnp.concatenate(
                [dg(table[1 + k], back[ch, f, :, PART:BACK], 0, 0) for k in range(3)], 1
            )
        total = dg(blksel[f], value.astype(BF16), 1, 1).astype(BF16)
        for k in range(4):
            blocks[a, 4 * f + k] = total[k * BROWS : (k + 1) * BROWS, :]

        def body(k):
            @pl.when(block_owner(k) != d)
            def _():
                hand_out(a, k).start()

            @pl.when(block_owner(k) == d)
            def _():
                frecv[a, z] = blocks[a, k]

        loop(4 * f, 4 * f + 4, body)

    inside = lax.div(z, 4) == c

    def finish(a, out_ref):
        @pl.when(inside)
        def _():
            handed(a, 7).wait_recv()

        @pl.when(jnp.logical_not(inside))
        def _():
            handed(a, 8).wait_recv()

        total = frecv[a, 0].astype(F32)
        for zz in range(1, 8):
            total += frecv[a, zz].astype(F32)
        out_ref[...] = total[0:BLK, :].astype(BF16)

    def store(o, le, n):
        out = (gg_hbm, gu_hbm, gd_hbm)[n]
        e = expert_of(o, le)
        return pltpu.make_async_copy(grads.at[n, e], out.at[e], out_sem.at[n])

    def weight_grads(o):
        def body(le):
            e = expert_of(o, le)
            r = of_expert(le)
            both = dg(rows[0, o, r, 0:D], ggu[o, r, :], 0, 0)
            grads[0, e] = both[:, 0:HID].astype(BF16)
            grads[1, e] = both[:, HID : 2 * HID].astype(BF16)
            grads[2, e] = dg(rows[1, o, r, 0:D], hid[o, r, :], 0, 0).astype(BF16)
            for n in range(3):
                store(o, le, n).start()

        loop(0, 2, body)

    first_hop(0, 0, 15)
    loop(0, 15, lambda j: dispatch(1, turn(j)).start())
    along_z(1, me).start()
    to_sibling(1, 0, me).start()
    for n, w in ((2, wgu), (3, wd)):
        all_rows = w.at[:, pl.ds(0, D)]
        pltpu.make_async_copy(all_rows, all_rows, in_sem.at[n]).wait()
    forward(0)
    outputs(0, 0)
    outputs(0, 1)
    second_hop(0)
    first_hop(1, 0, 5)
    forward(1)
    first_hop(1, 5, 10)
    outputs(1, 0)
    outputs(1, 1)
    reduce_near(0, 0)
    first_hop(1, 10, 15)
    backward(0)
    inputs(0, 0)
    inputs(0, 1)
    reduce_near(0, 1)
    reduce_far(0)
    reduce_far(1)
    reduce_near(1, 0)
    reduce_near(1, 1)
    second_hop(1)
    backward(1)
    inputs(1, 0)
    inputs(1, 1)
    reduce_near(2, 0)
    reduce_near(2, 1)
    combine(0, 0)
    combine(0, 1)
    weight_grads(0)
    weight_grads(1)
    combine(1, 0)
    combine(1, 1)
    finish(0, mixed_ref)
    finish(1, igrad_ref)
    told().wait_recv()
    total = dots[0]
    for k in range(1, 16):
        total += dots[k]
    dot = total[0:4, :]
    rgrad_ref[...] = dot - weights * jnp.sum(dot, 0, keepdims=True)

    told().wait_send()
    for f in range(2):
        across_all(f).wait_send()
        for ch in range(3):
            all_back(ch, f).wait_send()
    for a in range(2):
        fifteen = pl.ds(0, 15 * SLAB)
        pltpu.make_async_remote_copy(
            src_ref=send_slab.at[a, fifteen], dst_ref=cat.at[a, 0, c, fifteen],
            send_sem=xy_s.at[a], recv_sem=xy_r.at[a, 0],
            device_id=sib, device_id_type=MESH,
        ).wait_send()
        pltpu.make_async_remote_copy(
            src_ref=cat.at[a, 0, c], dst_ref=cat.at[a, 1, c],
            send_sem=zf_s.at[a], recv_sem=zf_r.at[a, 0],
            device_id=sib, device_id_type=MESH,
        ).wait_send()
        pltpu.make_async_remote_copy(
            src_ref=part.at[a, 1], dst_ref=crecv.at[a],
            send_sem=rc_s.at[a], recv_sem=rc_r.at[a, 0, 0],
            device_id=sib, device_id_type=MESH,
        ).wait_send()
        for f in range(2):
            from_sibling(a, f).wait_send()

        @pl.when(inside)
        def _():
            handed(a, 7).wait_send()

        @pl.when(jnp.logical_not(inside))
        def _():
            handed(a, 8).wait_send()

    for n, out in enumerate((gg_hbm, gu_hbm, gd_hbm)):
        pltpu.make_async_copy(grads.at[n], out, out_sem.at[n]).wait()


def deliver(
    mixed_in, igrad_in, rgrad_in, gg_in, gu_in, gd_in,
    mixed_out, igrad_out, rgrad_out, gg_out, gu_out, gd_out, sem,
):
    pairs = ((gg_in, gg_out), (gu_in, gu_out), (gd_in, gd_out))
    writes = []
    for n, (src, dst) in enumerate(pairs):
        for e in range(4):
            writes.append(pltpu.make_async_copy(src.at[e], dst.at[e], sem.at[n, e]))
    for write in writes:
        write.start()
    mixed_out[...] = mixed_in[...]
    igrad_out[...] = igrad_in[...]
    rgrad_out[...] = rgrad_in[...]
    for write in writes:
        write.wait()


def on_device(tokens, output_grad, router_logits, expert_ids, w_gate, w_up, w_down):
    anywhere = pl.BlockSpec(memory_space=pl.ANY)
    vmem = pl.BlockSpec(memory_space=pltpu.VMEM)
    dma = pltpu.SemaphoreType.DMA
    weight = jax.ShapeDtypeStruct((4, D, HID), BF16)
    kept = pltpu.VMEM((4, D, HID), BF16)
    part_kept = pltpu.VMEM((BLK, TOK), BF16)
    block = jax.ShapeDtypeStruct((BLK, TOK), BF16)
    mixed, igrad, rgrad, gg, gu, gd = pl.pallas_call(
        kernel,
        out_shape=(part_kept, part_kept, pltpu.VMEM((4, TOK), F32), kept, kept, kept),
        in_specs=[anywhere, anywhere, vmem, vmem, anywhere, anywhere, anywhere],
        out_specs=(vmem, vmem, vmem, anywhere, anywhere, anywhere),
        scratch_shapes=[
            pltpu.VMEM((PADDED, TOK), BF16),
            pltpu.VMEM((PADDED, TOK), BF16),
            pltpu.VMEM((4, D + WIDE - HALF, 2 * HID), BF16),
            pltpu.VMEM((4, D + WIDE - HALF, HID), BF16),
            pltpu.VMEM((2, 256, MSG), BF16),
            pltpu.VMEM((2, 2, 2, 256, MSG), BF16),
            pltpu.VMEM((2, 2, PAIR, PADDED), BF16),
            pltpu.VMEM((256, TOK), BF16),
            pltpu.VMEM((256, 3 * TOK), BF16),
            pltpu.VMEM((2, 4, 256, TOK), BF16),
            pltpu.VMEM((2, 4, 256, TOK), BF16),
            pltpu.VMEM((4, 256, TOK), BF16),
            pltpu.VMEM((4, PAIR, 256), BF16),
            pltpu.VMEM((4, 256, PAIR), BF16),
            pltpu.VMEM((2, 4 * BROWS, PART), BF16),
            pltpu.VMEM((2, PAIR, HID), F32),
            pltpu.VMEM((2, PAIR, HID), F32),
            pltpu.VMEM((2, PAIR, HID), F32),
            pltpu.VMEM((2, PAIR, HID), F32),
            pltpu.VMEM((2, PAIR, HID), BF16),
            pltpu.VMEM((2, PAIR, 2 * HID), BF16),
            pltpu.VMEM((2, PAIR, HID), F32),
            pltpu.VMEM((2, 2, 2, 2, PAIR, PART), BF16),
            pltpu.VMEM((2, 2, 2, PAIR, PART), BF16),
            pltpu.VMEM((2, 2, ROWS, PART), BF16),
            pltpu.VMEM((2, 2, ROWS, PART), BF16),
            pltpu.VMEM((3, 2, 256, BACK), BF16),
            pltpu.VMEM((3, 2, 256, BACK), BF16),
            pltpu.VMEM((2, 8, BROWS, TOK), BF16),
            pltpu.VMEM((2, 8, BROWS, TOK), BF16),
            pltpu.VMEM((16, 8, TOK), F32),
            pltpu.VMEM((3, 4, D, HID), BF16),
            dma((4,)),
            dma((2,)), dma((2, 16)),
            dma((2,)), dma((2, 2)),
            dma((2, 2)), dma((2, 2)),
            dma((2,)), dma((2, 2, 2)),
            dma(()), dma((2,)),
            dma((3, 2)), dma((3, 2)),
            dma((2,)), dma((2,)),
            dma(()), dma(()),
            dma((3,)),
        ],
        compiler_params=pltpu.CompilerParams(
            collective_id=0, has_side_effects=True, vmem_limit_bytes=59 * 2**20
        ),
        cost_estimate=pl.CostEstimate(
            flops=2 * 9 * 640 * D * HID, bytes_accessed=9 * 10**6, transcendentals=640 * HID
        ),
        name="moe_layer",
    )(
        tokens.T, output_grad.T, router_logits.T, expert_ids.T,
        w_gate, w_up, jnp.swapaxes(w_down, 1, 2),
    )
    mixed, igrad, rgrad, gg, gu, gd = pl.pallas_call(
        deliver,
        out_shape=(block, block, jax.ShapeDtypeStruct((4, TOK), F32), weight, weight, weight),
        in_specs=[vmem, vmem, vmem, vmem, vmem, vmem],
        out_specs=(vmem, vmem, vmem, anywhere, anywhere, anywhere),
        scratch_shapes=[dma((3, 4))],
        compiler_params=pltpu.CompilerParams(vmem_limit_bytes=16 * 2**20),
        cost_estimate=pl.CostEstimate(flops=0, bytes_accessed=9 * 10**6, transcendentals=0),
        name="deliver",
    )(mixed, igrad, rgrad, gg, gu, gd)
    return mixed.T, igrad.T, rgrad.T, gg, gu, jnp.swapaxes(gd, 1, 2)


def solution(mesh):
    in_specs = (
        P("expert", None),
        P("expert", None),
        P("expert", None),
        P("expert", None),
        P("expert", None, "dp"),
        P("expert", None, "dp"),
        P("expert", "dp", None),
    )
    out_specs = (
        P("expert", "dp"),
        P("expert", "dp"),
        P("expert", None),
        P("expert", None, "dp"),
        P("expert", None, "dp"),
        P("expert", "dp", None),
    )
    return jax.shard_map(
        on_device, mesh=mesh, in_specs=in_specs, out_specs=out_specs, check_vma=False
    )
```

```python
import jax
import jax.numpy as jnp
import numpy as np
from jax import lax
from jax.experimental import pallas as pl
from jax.experimental.pallas import tpu as pltpu
from jax.sharding import PartitionSpec as P

MESH = pl.DeviceIdType.MESH
F32 = jnp.float32
BF16 = jnp.bfloat16

D = 1440
HALF = 720
WIDE = 768
PADDED = 1536
HID = 128
TOK = 128
RANKS = 10
SRC = 16
ROWS = SRC * RANKS
PAIR = 2 * ROWS
SLAB = 16
MSG = 1024
GROUP = 256
PART = 384
STEP = 352
BACK = 512
DOT_LANE = 376
ORDER = (1, 12, 3, 4, 2, 8, 5, 15, 7, 13, 6, 14, 9, 11, 10)
FIRST = int(np.int32(np.uint32(sum(i << (4 * j) for j, i in enumerate(ORDER[:8])))))
LAST = sum(i << (4 * j) for j, i in enumerate(ORDER[8:]))
BLK = 90
BROWS = 96


def dg(a, b, ca, cb):
    return lax.dot_general(a, b, (((ca,), (cb,)), ((), ())), preferred_element_type=F32)


def iota(shape, dim):
    return lax.broadcasted_iota(jnp.int32, shape, dim)


def ones_where(mask):
    return jnp.where(mask, 1.0, 0.0).astype(BF16)


def kernel(
    tok_hbm, og_hbm, logits_ref, ids_ref, wg_hbm, wu_hbm, wd_hbm,
    mixed_ref, igrad_ref, rgrad_ref, gg_hbm, gu_hbm, gd_hbm,
    tok, og, wgu, wd,
    send_slab, cat, rows, sel_main, sel_fold, comb_hi, comb_lo, comb_one,
    grp, ungrp, blksel,
    sig, pre, act, upp, hid, ggu, dotc,
    part, crecv, zsend, zrecv, slab, back, blocks, frecv, dots,
    grads,
    in_sem, xy_s, xy_r, zf_s, zf_r, cf_s, cf_r, rc_s, rc_r, rz_s, rz_r,
    bk_s, bk_r, fb_s, fb_r, dt_s, dt_r, out_sem,
):
    d = lax.axis_index("dp")
    me = lax.axis_index("expert")
    z, c = lax.div(d, 2), lax.rem(d, 2)
    x, y = lax.div(me, 4), lax.rem(me, 4)
    par = lax.rem(z, 2)
    sib = (z * 2 + 1 - c, me)
    up = (lax.rem(z + 1, 8) * 2 + c, me)
    down = (lax.rem(z + 7, 8) * 2 + c, me)

    def peer(i):
        return lax.rem(x + i // 4, 4) * 4 + lax.rem(y + i % 4, 4)

    def origin(i):
        return lax.rem(x + 4 - i // 4, 4) * 4 + lax.rem(y + 4 - i % 4, 4)

    def slab_rows(s):
        return pl.ds(pl.multiple_of(s * SLAB, SLAB), SLAB)

    barrier = pltpu.get_barrier_semaphore()

    def greet(i, carry):
        pl.semaphore_signal(barrier, inc=1, device_id=(d, peer(i)), device_id_type=MESH)
        pl.semaphore_signal(
            barrier, inc=1, device_id=(lax.rem(d + i, 16), me), device_id_type=MESH
        )
        return carry

    lax.fori_loop(1, 16, greet, 0)

    loads = [
        pltpu.make_async_copy(tok_hbm, tok.at[pl.ds(0, D)], in_sem.at[0]),
        pltpu.make_async_copy(og_hbm, og.at[pl.ds(0, D)], in_sem.at[1]),
    ]
    for e in range(4):
        for n, src, dst in (
            (2, wg_hbm, wgu.at[e, pl.ds(0, D), pl.ds(0, HID)]),
            (2, wu_hbm, wgu.at[e, pl.ds(0, D), pl.ds(HID, HID)]),
            (3, wd_hbm, wd.at[e, pl.ds(0, D)]),
        ):
            loads.append(pltpu.make_async_copy(src.at[e], dst, in_sem.at[n]))
    loads[0].start()
    loads[1].start()
    tok[pl.ds(D, PADDED - D), :] = jnp.zeros((PADDED - D, TOK), BF16)
    og[pl.ds(D, PADDED - D), :] = jnp.zeros((PADDED - D, TOK), BF16)

    lifted = jnp.exp(logits_ref[...])
    weights = lifted / jnp.sum(lifted, 0, keepdims=True)
    ids = ids_ref[...]
    row = iota((256, TOK), 0)
    spot = row & 15
    earlier = ones_where(iota((TOK, TOK), 0) < iota((TOK, TOK), 1))

    def select(expert, rank):
        named = jnp.zeros((256, TOK), F32)
        weigh = jnp.zeros((256, TOK), F32)
        for p in range(4):
            same = ids[p : p + 1, :] == expert
            named = jnp.where(same, 1.0, named)
            weigh = jnp.where(same, weights[p : p + 1, :], weigh)
        before = dg(named.astype(BF16), earlier, 1, 0)
        chosen = (before == rank.astype(F32)) & (named > 0.5)
        return chosen, jnp.where(chosen, weigh, 0.0)

    second = jnp.where(spot >= RANKS, 1, 0)
    base = 4 * (row >> 4) + 2 * par
    main_expert = base + second
    fold_expert = base + 1
    base_back = 4 * (row >> 4) + 2 * (1 - par)
    main_back = base_back + second
    fold_back = base_back + 1
    main, main_w = select(main_expert, spot - RANKS * second)
    fold, fold_w = select(fold_expert, 6 + (spot & 3))
    sel_main[...] = ones_where(main)
    for k in range(3):
        sel_fold[:, k * TOK : (k + 1) * TOK] = ones_where(fold & ((spot >> 2) == k))
    start = pl.multiple_of(c * WIDE, WIDE)

    def gather(a, source):
        loads[a].wait()
        whole = dg(sel_main[...], source[pl.ds(start, WIDE), :], 1, 1)
        folded = jnp.zeros((256, GROUP), F32)
        for k in range(3):
            feats = source[pl.ds(pl.multiple_of(start + k * GROUP, GROUP), GROUP), :]
            folded += dg(sel_fold[:, k * TOK : (k + 1) * TOK], feats, 1, 1)
        if a == 1:
            whole = jnp.sum(main_w, 1, keepdims=True) * whole
            some = jnp.where((spot >> 2) < 3, fold_w, 0.0)
            folded = jnp.sum(some, 1, keepdims=True) * folded
        send_slab[a, :, 0:WIDE] = whole.astype(BF16)
        send_slab[a, :, WIDE:MSG] = folded.astype(BF16)

    def dispatch(a, i):
        return pltpu.make_async_remote_copy(
            src_ref=send_slab.at[a, slab_rows(peer(i))],
            dst_ref=cat.at[a, 0, c, slab_rows(me)],
            send_sem=xy_s.at[a], recv_sem=xy_r.at[a, i],
            device_id=(d, peer(i)), device_id_type=MESH,
        )

    def arrive(a, i):
        return pltpu.make_async_remote_copy(
            src_ref=send_slab.at[a, slab_rows(peer(i))],
            dst_ref=cat.at[a, 0, c, slab_rows(origin(i))],
            send_sem=xy_s.at[a], recv_sem=xy_r.at[a, i],
            device_id=(d, peer(i)), device_id_type=MESH,
        )

    def along_z(a, s):
        side = s // 8
        return pltpu.make_async_remote_copy(
            src_ref=cat.at[a, 0, c, slab_rows(s)],
            dst_ref=cat.at[a, 1, c, slab_rows(s)],
            send_sem=zf_s.at[a], recv_sem=zf_r.at[a, side],
            device_id=(lax.rem(z + 1 - 2 * side + 8, 8) * 2 + c, me), device_id_type=MESH,
        )

    def along_z_all(a, side):
        eight = pl.ds(8 * SLAB * side, 8 * SLAB)
        return pltpu.make_async_remote_copy(
            src_ref=cat.at[a, 0, c, eight], dst_ref=cat.at[a, 1, c, eight],
            send_sem=zf_s.at[a], recv_sem=zf_r.at[a, side],
            device_id=down if side else up, device_id_type=MESH,
        )

    def to_sibling(a, o, s, count=1):
        some = pl.ds(pl.multiple_of(s * SLAB, SLAB), count * SLAB)
        return pltpu.make_async_remote_copy(
            src_ref=cat.at[a, o, c, some], dst_ref=cat.at[a, o, c, some],
            send_sem=cf_s.at[a, o], recv_sem=cf_r.at[a, o],
            device_id=sib, device_id_type=MESH,
        )

    def from_sibling(a, o):
        return pltpu.make_async_remote_copy(
            src_ref=cat.at[a, o, c], dst_ref=cat.at[a, o, 1 - c],
            send_sem=cf_s.at[a, o], recv_sem=cf_r.at[a, o],
            device_id=sib, device_id_type=MESH,
        )

    def loop(lo, hi, body):
        def step(i, carry):
            body(i)
            return carry

        lax.fori_loop(lo, hi, step, 0)

    def turn(j):
        return (jnp.where(j < 8, FIRST, LAST) >> (4 * lax.rem(j, 8))) & 15

    gather(0, tok)
    pl.semaphore_wait(barrier, 30)
    loop(0, 15, lambda j: dispatch(0, turn(j)).start())
    cat[0, 0, c, slab_rows(me), :] = send_slab[0, slab_rows(me), :]
    along_z(0, me).start()
    to_sibling(0, 0, me).start()
    for load in loads[2:]:
        load.start()
    gather(1, og)
    cat[1, 0, c, slab_rows(me), :] = send_slab[1, slab_rows(me), :]

    for e in range(4):
        wgu[e, pl.ds(D, WIDE - HALF), :] = jnp.zeros((WIDE - HALF, 2 * HID), BF16)
        wd[e, pl.ds(D, WIDE - HALF), :] = jnp.zeros((WIDE - HALF, HID), BF16)
    main, main_w = select(main_back, spot - RANKS * second)
    fold, fold_w = select(fold_back, 6 + (spot & 3))
    comb_hi[0] = main_w.astype(BF16)
    comb_lo[0] = (main_w - main_w.astype(BF16).astype(F32)).astype(BF16)
    comb_one[0] = ones_where(main)
    for k in range(3):
        here = (spot >> 2) == k
        w_here = jnp.where(here, fold_w, 0.0)
        comb_hi[1 + k] = w_here.astype(BF16)
        comb_lo[1 + k] = (w_here - w_here.astype(BF16).astype(F32)).astype(BF16)
        comb_one[1 + k] = ones_where(fold & here)

    n = iota((PAIR, 256), 0)
    i = iota((PAIR, 256), 1)
    later = jnp.where(n >= ROWS, 1, 0)
    m = n - ROWS * later
    s = (m * 6554) >> 16
    q = m - RANKS * s + RANKS * later
    grp[0] = ones_where((i == s * SLAB + q) & (q < 16))
    for k in range(3):
        grp[1 + k] = ones_where((i == s * SLAB + 4 * k + q - 16) & (q >= 16))
    n = iota((256, PAIR), 1)
    i = iota((256, PAIR), 0)
    later = jnp.where(n >= ROWS, 1, 0)
    m = n - ROWS * later
    s = (m * 6554) >> 16
    q = m - RANKS * s + RANKS * later
    ungrp[0] = ones_where((i == s * SLAB + q) & (q < 16))
    for k in range(3):
        ungrp[1 + k] = ones_where((i == s * SLAB + 4 * k + q - 16) & (q >= 16))
    line = iota((4 * BROWS, PART), 0)
    block = (line * 683) >> 16
    inner = line - BROWS * block
    place = BLK * block + inner
    for f in range(2):
        blksel[f] = ones_where((iota((4 * BROWS, PART), 1) == place + 8 * f) & (inner < BLK))

    def first_hop(a, lo, hi):
        def body(j):
            i = turn(j)
            arrive(a, i).wait_recv()

            along_z(a, origin(i)).start()
            to_sibling(a, 0, origin(i)).start()

        loop(lo, hi, body)

    def second_hop(a):
        for side in range(2):
            along_z_all(a, side).wait_recv()
            to_sibling(a, 1, 8 * side, 8).start()

    def regroup(a, o):
        from_sibling(a, o).wait_recv()
        for h in range(2):
            folded = cat[a, o, h, :, WIDE:MSG]
            for k in range(3):
                value = dg(grp[0], cat[a, o, h, :, k * GROUP : (k + 1) * GROUP], 1, 0)
                value += dg(grp[1 + k], folded, 1, 0)
                rows[a, o, :, h * WIDE + k * GROUP : h * WIDE + (k + 1) * GROUP] = value.astype(BF16)

    def expert_of(o, le):
        return 2 * (par + o - 2 * par * o) + le

    def of_expert(le):
        return pl.ds(pl.multiple_of(le * ROWS, ROWS), ROWS)

    def feats(far, f):
        side = 1 - c if far else c
        return pl.ds(pl.multiple_of(side * HALF + f * STEP, 16), PART)

    def to_core(a, f, o):
        return pltpu.make_async_remote_copy(
            src_ref=part.at[a, 1, f, o], dst_ref=crecv.at[a, f, o],
            send_sem=rc_s.at[a], recv_sem=rc_r.at[a, f, o],
            device_id=sib, device_id_type=MESH,
        )

    def forward(o):
        regroup(0, o)

        def body(le):
            e = expert_of(o, le)
            r = of_expert(le)
            xe = rows[0, o, r, 0:D]
            both = dg(xe, wgu[e, pl.ds(0, D), :], 1, 0)
            pg = both[:, 0:HID]
            pu = both[:, HID : 2 * HID] + 1.0
            sg = jax.nn.sigmoid(1.702 * pg)
            ac = pg * sg
            sig[o, r, :] = sg
            pre[o, r, :] = pg
            act[o, r, :] = ac
            upp[o, r, :] = pu
            hid[o, r, :] = (ac * pu).astype(BF16)

        loop(0, 2, body)

    def outputs(o, f):
        def body(le):
            e = expert_of(o, le)
            r = of_expert(le)
            for far in range(2):
                value = dg(hid[o, r, :], wd[e, feats(far, f), :], 1, 1)
                part[0, far, f, o, r, :] = value.astype(BF16)

        loop(0, 2, body)
        to_core(0, f, o).start()

    def backward(o):
        regroup(1, o)

        def body(le):
            e = expert_of(o, le)
            r = of_expert(le)
            ge = rows[1, o, r, 0:D]
            hg = dg(ge, wd[e, pl.ds(0, D), :], 1, 0)
            sg, pg, ac, pu = sig[o, r, :], pre[o, r, :], act[o, r, :], upp[o, r, :]
            slope = sg + 1.702 * pg * sg * (1.0 - sg)
            ggu[o, r, 0:HID] = (hg * pu * slope).astype(BF16)
            ggu[o, r, HID : 2 * HID] = (hg * ac).astype(BF16)
            dot = jnp.sum(hid[o, r, :].astype(F32) * hg, 1, keepdims=True)
            dotc[o, r, :] = jnp.broadcast_to(dot, (ROWS, HID))

        loop(0, 2, body)

    def inputs(o, f):
        def body(le):
            e = expert_of(o, le)
            r = of_expert(le)
            for far in range(2):
                value = dg(ggu[o, r, :], wgu[e, feats(far, f), :], 1, 1)
                if f == 1:
                    dot = dotc[o, r, 0:1] if far == 0 else 0.0
                    value = jnp.where(iota((ROWS, PART), 1) == DOT_LANE, dot, value)
                part[1, far, f, o, r, :] = value.astype(BF16)

        loop(0, 2, body)
        to_core(1, f, o).start()

    def across(a, f, le):
        return pltpu.make_async_remote_copy(
            src_ref=zsend.at[a, f, le], dst_ref=zrecv.at[a, f, le],
            send_sem=rz_s.at[a], recv_sem=rz_r.at[a, f],
            device_id=up if le == 0 else down, device_id_type=MESH,
        )

    def reduce_far(a, f):
        to_core(a, f, 0).wait_recv()
        for le in range(2):
            r = pl.ds(le * ROWS, ROWS)
            total = part[a, 0, f, 0, r, :].astype(F32) + crecv[a, f, 0, r, :].astype(F32)
            zsend[a, f, le] = total.astype(BF16)
            across(a, f, le).start()

    def give_back(a, f, i):
        return pltpu.make_async_remote_copy(
            src_ref=slab.at[a, f, slab_rows(peer(i))],
            dst_ref=back.at[a, f, slab_rows(me)],
            send_sem=bk_s.at[a, f], recv_sem=bk_r.at[a, f],
            device_id=(d, peer(i)), device_id_type=MESH,
        )

    def all_back(a, f):
        fifteen = pl.ds(0, 15 * SLAB)
        return pltpu.make_async_remote_copy(
            src_ref=slab.at[a, f, fifteen], dst_ref=back.at[a, f, fifteen],
            send_sem=bk_s.at[a, f], recv_sem=bk_r.at[a, f],
            device_id=sib, device_id_type=MESH,
        )

    def reduce_near(a, f):
        to_core(a, f, 1).wait_recv()
        totals = []
        pltpu.make_async_remote_copy(
            src_ref=zsend.at[a, f], dst_ref=zrecv.at[a, f],
            send_sem=rz_s.at[a], recv_sem=rz_r.at[a, f],
            device_id=up, device_id_type=MESH,
        ).wait_recv()
        for le in range(2):
            r = pl.ds(le * ROWS, ROWS)
            total = part[a, 0, f, 1, r, :].astype(F32) + crecv[a, f, 1, r, :].astype(F32)
            totals.append((total + zrecv[a, f, le].astype(F32)).astype(BF16))
        both = jnp.concatenate(totals, 0)
        slab[a, f, :, 0:PART] = dg(ungrp[0], both, 1, 0).astype(BF16)
        folded = jnp.zeros((256, TOK), F32)
        for k in range(3):
            folded += dg(ungrp[1 + k], both[:, k * TOK : (k + 1) * TOK], 1, 0)
        slab[a, f, :, PART:BACK] = folded.astype(BF16)
        back[a, f, slab_rows(me), :] = slab[a, f, slab_rows(me), :]
        loop(0, 15, lambda j: give_back(a, f, turn(14 - j)).start())

    def block_owner(k):
        return (4 * c + k // 2) * 2 + k % 2

    def hand_out(a, k):
        return pltpu.make_async_remote_copy(
            src_ref=blocks.at[a, k], dst_ref=frecv.at[a, z],
            send_sem=fb_s.at[a], recv_sem=fb_r.at[a],
            device_id=(block_owner(k), me), device_id_type=MESH,
        )

    def handed(a, count):
        return pltpu.make_async_remote_copy(
            src_ref=blocks.at[a, pl.ds(0, count)], dst_ref=frecv.at[a, pl.ds(0, count)],
            send_sem=fb_s.at[a], recv_sem=fb_r.at[a],
            device_id=sib, device_id_type=MESH,
        )

    def tell(i):
        return pltpu.make_async_remote_copy(
            src_ref=dots.at[d], dst_ref=dots.at[d],
            send_sem=dt_s, recv_sem=dt_r,
            device_id=(lax.rem(d + i, 16), me), device_id_type=MESH,
        )

    def told():
        return pltpu.make_async_remote_copy(
            src_ref=dots.at[pl.ds(0, 15)], dst_ref=dots.at[pl.ds(0, 15)],
            send_sem=dt_s, recv_sem=dt_r,
            device_id=sib, device_id_type=MESH,
        )

    def combine(a, f):
        all_back(a, f).wait_recv()
        if a == 1 and f == 1:
            main_dot = back[1, 1, :, DOT_LANE : DOT_LANE + 1].astype(F32)
            lane = DOT_LANE + TOK
            fold_dot = back[1, 1, :, lane : lane + 1].astype(F32)
            main_dot = jnp.where(comb_one[0].astype(F32) > 0.5, main_dot, 0.0)
            fold_dot = jnp.where(comb_one[3].astype(F32) > 0.5, fold_dot, 0.0)
            lines = []
            for p in range(4):
                mine_p = jnp.where(ids[p : p + 1, :] == main_back, main_dot, 0.0)
                mine_p += jnp.where(ids[p : p + 1, :] == fold_back, fold_dot, 0.0)
                lines.append(jnp.sum(mine_p, 0, keepdims=True))
            dots[d] = jnp.concatenate(lines + [jnp.zeros((4, TOK), F32)], 0)
            loop(1, 16, lambda i: tell(i).start())
        tables = (comb_hi, comb_lo) if a == 0 else (comb_one,)
        value = jnp.zeros((TOK, PART), F32)
        for table in tables:
            value += dg(table[0], back[a, f, :, 0:PART], 0, 0)
            value += jnp.concatenate(
                [dg(table[1 + k], back[a, f, :, PART:BACK], 0, 0) for k in range(3)], 1
            )
        total = dg(blksel[f], value.astype(BF16), 1, 1).astype(BF16)
        for k in range(4):
            blocks[a, 4 * f + k] = total[k * BROWS : (k + 1) * BROWS, :]

        def body(k):
            @pl.when(block_owner(k) != d)
            def _():
                hand_out(a, k).start()

            @pl.when(block_owner(k) == d)
            def _():
                frecv[a, z] = blocks[a, k]

        loop(4 * f, 4 * f + 4, body)

    inside = lax.div(z, 4) == c

    def finish(a, out_ref):
        @pl.when(inside)
        def _():
            handed(a, 7).wait_recv()

        @pl.when(jnp.logical_not(inside))
        def _():
            handed(a, 8).wait_recv()

        total = frecv[a, 0].astype(F32)
        for zz in range(1, 8):
            total += frecv[a, zz].astype(F32)
        out_ref[...] = total[0:BLK, :].astype(BF16)

    def store(o, le, n):
        out = (gg_hbm, gu_hbm, gd_hbm)[n]
        e = expert_of(o, le)
        return pltpu.make_async_copy(grads.at[n, e], out.at[e], out_sem.at[n])

    def weight_grads(o):
        def body(le):
            e = expert_of(o, le)
            r = of_expert(le)
            both = dg(rows[0, o, r, 0:D], ggu[o, r, :], 0, 0)
            grads[0, e] = both[:, 0:HID].astype(BF16)
            grads[1, e] = both[:, HID : 2 * HID].astype(BF16)
            grads[2, e] = dg(rows[1, o, r, 0:D], hid[o, r, :], 0, 0).astype(BF16)
            for n in range(3):
                store(o, le, n).start()

        loop(0, 2, body)

    first_hop(0, 0, 15)
    loop(0, 15, lambda j: dispatch(1, turn(j)).start())
    along_z(1, me).start()
    to_sibling(1, 0, me).start()
    for n, w in ((2, wgu), (3, wd)):
        all_rows = w.at[:, pl.ds(0, D)]
        pltpu.make_async_copy(all_rows, all_rows, in_sem.at[n]).wait()
    forward(0)
    outputs(0, 0)
    outputs(0, 1)
    second_hop(0)
    first_hop(1, 0, 5)
    reduce_far(0, 0)
    reduce_far(0, 1)
    forward(1)
    first_hop(1, 5, 10)
    outputs(1, 0)
    outputs(1, 1)
    first_hop(1, 10, 15)
    backward(0)
    inputs(0, 0)
    inputs(0, 1)
    reduce_near(0, 0)
    reduce_near(0, 1)
    reduce_far(1, 0)
    reduce_far(1, 1)
    weight_grads(0)
    second_hop(1)
    backward(1)
    inputs(1, 0)
    inputs(1, 1)
    reduce_near(1, 0)
    reduce_near(1, 1)
    combine(0, 0)
    combine(0, 1)
    weight_grads(1)
    combine(1, 0)
    combine(1, 1)
    finish(0, mixed_ref)
    finish(1, igrad_ref)
    told().wait_recv()
    total = dots[0]
    for k in range(1, 16):
        total += dots[k]
    dot = total[0:4, :]
    rgrad_ref[...] = dot - weights * jnp.sum(dot, 0, keepdims=True)

    told().wait_send()
    for a in range(2):
        fifteen = pl.ds(0, 15 * SLAB)
        pltpu.make_async_remote_copy(
            src_ref=send_slab.at[a, fifteen], dst_ref=cat.at[a, 0, c, fifteen],
            send_sem=xy_s.at[a], recv_sem=xy_r.at[a, 0],
            device_id=sib, device_id_type=MESH,
        ).wait_send()
        pltpu.make_async_remote_copy(
            src_ref=cat.at[a, 0, c], dst_ref=cat.at[a, 1, c],
            send_sem=zf_s.at[a], recv_sem=zf_r.at[a, 0],
            device_id=sib, device_id_type=MESH,
        ).wait_send()
        pltpu.make_async_remote_copy(
            src_ref=part.at[a, 1], dst_ref=crecv.at[a],
            send_sem=rc_s.at[a], recv_sem=rc_r.at[a, 0, 0],
            device_id=sib, device_id_type=MESH,
        ).wait_send()
        pltpu.make_async_remote_copy(
            src_ref=zsend.at[a], dst_ref=zrecv.at[a],
            send_sem=rz_s.at[a], recv_sem=rz_r.at[a, 0],
            device_id=sib, device_id_type=MESH,
        ).wait_send()
        for f in range(2):
            from_sibling(a, f).wait_send()
            all_back(a, f).wait_send()

        @pl.when(inside)
        def _():
            handed(a, 7).wait_send()

        @pl.when(jnp.logical_not(inside))
        def _():
            handed(a, 8).wait_send()

    for n, out in enumerate((gg_hbm, gu_hbm, gd_hbm)):
        pltpu.make_async_copy(grads.at[n], out, out_sem.at[n]).wait()


def deliver(
    mixed_in, igrad_in, rgrad_in, gg_in, gu_in, gd_in,
    mixed_out, igrad_out, rgrad_out, gg_out, gu_out, gd_out, sem,
):
    pairs = ((gg_in, gg_out), (gu_in, gu_out), (gd_in, gd_out))
    writes = []
    for n, (src, dst) in enumerate(pairs):
        for e in range(4):
            writes.append(pltpu.make_async_copy(src.at[e], dst.at[e], sem.at[n, e]))
    for write in writes:
        write.start()
    mixed_out[...] = mixed_in[...]
    igrad_out[...] = igrad_in[...]
    rgrad_out[...] = rgrad_in[...]
    for write in writes:
        write.wait()


def on_device(tokens, output_grad, router_logits, expert_ids, w_gate, w_up, w_down):
    anywhere = pl.BlockSpec(memory_space=pl.ANY)
    vmem = pl.BlockSpec(memory_space=pltpu.VMEM)
    dma = pltpu.SemaphoreType.DMA
    weight = jax.ShapeDtypeStruct((4, D, HID), BF16)
    kept = pltpu.VMEM((4, D, HID), BF16)
    part_kept = pltpu.VMEM((BLK, TOK), BF16)
    block = jax.ShapeDtypeStruct((BLK, TOK), BF16)
    mixed, igrad, rgrad, gg, gu, gd = pl.pallas_call(
        kernel,
        out_shape=(part_kept, part_kept, pltpu.VMEM((4, TOK), F32), kept, kept, kept),
        in_specs=[anywhere, anywhere, vmem, vmem, anywhere, anywhere, anywhere],
        out_specs=(vmem, vmem, vmem, anywhere, anywhere, anywhere),
        scratch_shapes=[
            pltpu.VMEM((PADDED, TOK), BF16),
            pltpu.VMEM((PADDED, TOK), BF16),
            pltpu.VMEM((4, D + WIDE - HALF, 2 * HID), BF16),
            pltpu.VMEM((4, D + WIDE - HALF, HID), BF16),
            pltpu.VMEM((2, 256, MSG), BF16),
            pltpu.VMEM((2, 2, 2, 256, MSG), BF16),
            pltpu.VMEM((2, 2, PAIR, PADDED), BF16),
            pltpu.VMEM((256, TOK), BF16),
            pltpu.VMEM((256, 3 * TOK), BF16),
            pltpu.VMEM((4, 256, TOK), BF16),
            pltpu.VMEM((4, 256, TOK), BF16),
            pltpu.VMEM((4, 256, TOK), BF16),
            pltpu.VMEM((4, PAIR, 256), BF16),
            pltpu.VMEM((4, 256, PAIR), BF16),
            pltpu.VMEM((2, 4 * BROWS, PART), BF16),
            pltpu.VMEM((2, PAIR, HID), F32),
            pltpu.VMEM((2, PAIR, HID), F32),
            pltpu.VMEM((2, PAIR, HID), F32),
            pltpu.VMEM((2, PAIR, HID), F32),
            pltpu.VMEM((2, PAIR, HID), BF16),
            pltpu.VMEM((2, PAIR, 2 * HID), BF16),
            pltpu.VMEM((2, PAIR, HID), F32),
            pltpu.VMEM((2, 2, 2, 2, PAIR, PART), BF16),
            pltpu.VMEM((2, 2, 2, PAIR, PART), BF16),
            pltpu.VMEM((2, 2, 2, ROWS, PART), BF16),
            pltpu.VMEM((2, 2, 2, ROWS, PART), BF16),
            pltpu.VMEM((2, 2, 256, BACK), BF16),
            pltpu.VMEM((2, 2, 256, BACK), BF16),
            pltpu.VMEM((2, 8, BROWS, TOK), BF16),
            pltpu.VMEM((2, 8, BROWS, TOK), BF16),
            pltpu.VMEM((16, 8, TOK), F32),
            pltpu.VMEM((3, 4, D, HID), BF16),
            dma((4,)),
            dma((2,)), dma((2, 16)),
            dma((2,)), dma((2, 2)),
            dma((2, 2)), dma((2, 2)),
            dma((2,)), dma((2, 2, 2)),
            dma((2,)), dma((2, 2)),
            dma((2, 2)), dma((2, 2)),
            dma((2,)), dma((2,)),
            dma(()), dma(()),
            dma((3,)),
        ],
        compiler_params=pltpu.CompilerParams(
            collective_id=0, has_side_effects=True, vmem_limit_bytes=59 * 2**20
        ),
        cost_estimate=pl.CostEstimate(
            flops=2 * 9 * 640 * D * HID, bytes_accessed=9 * 10**6, transcendentals=640 * HID
        ),
        name="moe_layer",
    )(
        tokens.T, output_grad.T, router_logits.T, expert_ids.T,
        w_gate, w_up, jnp.swapaxes(w_down, 1, 2),
    )
    mixed, igrad, rgrad, gg, gu, gd = pl.pallas_call(
        deliver,
        out_shape=(block, block, jax.ShapeDtypeStruct((4, TOK), F32), weight, weight, weight),
        in_specs=[vmem, vmem, vmem, vmem, vmem, vmem],
        out_specs=(vmem, vmem, vmem, anywhere, anywhere, anywhere),
        scratch_shapes=[dma((3, 4))],
        compiler_params=pltpu.CompilerParams(vmem_limit_bytes=16 * 2**20),
        cost_estimate=pl.CostEstimate(flops=0, bytes_accessed=9 * 10**6, transcendentals=0),
        name="deliver",
    )(mixed, igrad, rgrad, gg, gu, gd)
    return mixed.T, igrad.T, rgrad.T, gg, gu, jnp.swapaxes(gd, 1, 2)


def solution(mesh):
    in_specs = (
        P("expert", None),
        P("expert", None),
        P("expert", None),
        P("expert", None),
        P("expert", None, "dp"),
        P("expert", None, "dp"),
        P("expert", "dp", None),
    )
    out_specs = (
        P("expert", "dp"),
        P("expert", "dp"),
        P("expert", None),
        P("expert", None, "dp"),
        P("expert", None, "dp"),
        P("expert", "dp", None),
    )
    return jax.shard_map(
        on_device, mesh=mesh, in_specs=in_specs, out_specs=out_specs, check_vma=False
    )
```
